32 devices in a mesh: dp: 8 (over y, x, core), tensor: 4 (over z).
Axes of the slice: x: 2, y: 2, z: 4, core: 2. Of those that a mesh axis runs over, the one named last changes fastest.
Arguments:
- tokens: bfloat16 [16384, 768], P('dp'), may hold values from -6 to 6
- segments: int32 [16384], P('dp'), may hold values from 0 to 3, as said below
- query_weight: bfloat16 [768, 768], P(None, 'tensor'), may hold values from -0.21875 to 0.21875
- key_weight: bfloat16 [768, 768], P(None, 'tensor'), may hold values from -0.21875 to 0.21875
- value_weight: bfloat16 [768, 768], P(None, 'tensor'), may hold values from -0.21875 to 0.21875
- query_bias: float32 [768], P('tensor'), may hold values from -3 to 3
- value_bias: float32 [768], P('tensor'), may hold values from -3 to 3
- output_weight: bfloat16 [768, 768], P('tensor'), may hold values from -3 to 3
- output_bias: float32 [768], replicated, may hold values from -3 to 3
- gain_one: float32 [768], replicated, may hold values from 0.25 to 1.75
- shift_one: float32 [768], replicated, may hold values from -3 to 3
- inner_weight: bfloat16 [768, 3072], P(None, 'tensor'), may hold values from -0.21875 to 0.21875
- inner_bias: float32 [3072], P('tensor'), may hold values from -3 to 3
- down_weight: bfloat16 [3072, 768], P('tensor'), may hold values from -0.109375 to 0.109375
- down_bias: float32 [768], replicated, may hold values from -3 to 3
- gain_two: float32 [768], replicated, may hold values from 0.25 to 1.75
- shift_two: float32 [768], replicated, may hold values from -3 to 3
- cotangent: bfloat16 [16384, 768], P('dp'), may hold values from -6 to 6
Outputs:
- layer_out: bfloat16 [16384, 768], P('dp')
- tokens_grad: float32 [16384, 768], P('dp')
- query_grad: float32 [768, 768], P(None, 'tensor')
- key_grad: float32 [768, 768], P(None, 'tensor')
- value_grad: float32 [768, 768], P(None, 'tensor')
- querybias_grad: float32 [768], P('tensor')
- valuebias_grad: float32 [768], P('tensor')
- output_grad: float32 [768, 768], P('tensor')
- outbias_grad: float32 [768], replicated
- gainone_grad: float32 [768], replicated
- shiftone_grad: float32 [768], replicated
- inner_grad: float32 [768, 3072], P(None, 'tensor')
- innerbias_grad: float32 [3072], P('tensor')
- down_grad: float32 [3072, 768], P('tensor')
- downbias_grad: float32 [768], replicated
- gaintwo_grad: float32 [768], replicated
- shifttwo_grad: float32 [768], replicated
The draws below stay inside these ranges and needn't reach their ends.
Inputs may be any that keep to these rules, and one draw needn't show every extreme that they name: `segments`: each document is a run of 204 to 2048 tokens, the last cut off at the end, and may cross sequence borders; documents are labelled 0, 1, 2, 3, 0, 1, ... in order, so that the documents that touch one sequence carry distinct labels.
All inputs are finite; a program needn't handle non-finite values.
Results may differ from the reference program's by a relative error of at most 0.014.
Values sent between devices are 32-bit elements; how exact they have to be, the bound alone decides.
No kernel may reach another device: no remote copies, remote signals or barrier semaphores. Data moves between devices by JAX's collectives and lax.ppermute only.
A program may use at most 128 MiB of HBM per device.

```python
import jax
import jax.numpy as jnp
from jax import lax

D = 768
HEADS = 12
HEAD_DIM = 64
FF = 3072
SEQ_LEN = 512
TOKENS = 16384


def draw_segments(key, part):
    key = jax.random.fold_in(key, 7)
    shortest = max(2, 2 * SEQ_LEN // 5)
    longest = 4 * SEQ_LEN
    number_docs = TOKENS // shortest + 2
    lengths = jax.random.randint(key, (number_docs,), shortest, longest + 1)
    starts = jnp.cumsum(lengths)
    places = jnp.arange(TOKENS, dtype=jnp.int32)
    counted = jnp.sum((starts[None, :] <= places[:, None]).astype(jnp.int32), axis=1).astype(jnp.int32)
    return (counted % 4).astype(jnp.int32)


def shard_levels(own_key, shape, pieces, smallest, high):
    level = 1.0
    for axis_at, blocks in pieces:
        heights = jax.random.uniform(jax.random.fold_in(jax.random.fold_in(own_key, 6), axis_at), (blocks,), jnp.float32, smallest / len(pieces), high / len(pieces))
        level = level * jnp.repeat(jnp.exp(heights), shape[axis_at] // blocks).reshape((-1,) + (1,) * (len(shape) - 1 - axis_at))
    return level


def noise(stream_key, extent, width, limit, cuts=(), kind=jnp.bfloat16):
    values = jax.random.normal(stream_key, extent, jnp.float32) * width
    if len(cuts) > 0:
        values = shard_levels(stream_key, extent, cuts, -0.22, 0.18) * values
    return jnp.clip(values, min=-limit, max=limit).astype(kind)


def setup_inputs(seed: int = 0) -> dict:
    splits = jax.random.split(jax.random.key(seed), 19)
    tokens = noise(splits[0], (TOKENS, D), 1.0, 6.0, ((0, 8),))
    segments = draw_segments(jax.random.fold_in(splits[18], 71), 0)
    query_weight = noise(splits[2], (D, D), D ** -0.5, 0.21875, ((1, 4),))
    key_weight = noise(splits[3], (D, D), D ** -0.5, 0.21875, ((1, 4),))
    value_weight = noise(splits[4], (D, D), D ** -0.5, 0.21875, ((1, 4),))
    query_bias = noise(splits[5], (D,), 0.5, 3.0, ((0, 4),), jnp.float32)
    value_bias = noise(splits[6], (D,), 0.5, 3.0, ((0, 4),), jnp.float32)
    output_weight = noise(splits[7], (D, D), (max(1, D // 192)) ** -0.5, 3.0, ((0, 4),))
    output_bias = noise(splits[8], (D,), 0.5, 3.0, (), jnp.float32)
    gain_one = jnp.clip(1.0 + 0.15 * jax.random.normal(splits[9], (D,), jnp.float32), 0.25, 1.75)
    shift_one = noise(splits[10], (D,), 0.5, 3.0, (), jnp.float32)
    inner_weight = noise(splits[11], (D, FF), D ** -0.5, 0.21875, ((1, 4),))
    inner_bias = noise(splits[12], (FF,), 0.5, 3.0, ((0, 4),), jnp.float32)
    down_weight = noise(splits[13], (FF, D), FF ** -0.5, 0.109375, ((0, 4),))
    down_bias = noise(splits[14], (D,), 0.5, 3.0, (), jnp.float32)
    gain_two = jnp.clip(1.0 + 0.15 * jax.random.normal(splits[15], (D,), jnp.float32), 0.25, 1.75)
    shift_two = noise(splits[16], (D,), 0.5, 3.0, (), jnp.float32)
    cotangent = noise(splits[17], (TOKENS, D), 1.0, 6.0, ((0, 8),))
    return dict(tokens=tokens, segments=segments, query_weight=query_weight, key_weight=key_weight, value_weight=value_weight, query_bias=query_bias, value_bias=value_bias, output_weight=output_weight, output_bias=output_bias, gain_one=gain_one, shift_one=shift_one, inner_weight=inner_weight, inner_bias=inner_bias, down_weight=down_weight, down_bias=down_bias, gain_two=gain_two, shift_two=shift_two, cotangent=cotangent)


@jax.custom_vjp
def low(v):
    return lax.optimization_barrier(v.astype(jnp.bfloat16)).astype(jnp.float32)

@jax.custom_vjp
def low_back(v):
    return v

def low_keep(v):
    return (low(v), None)

def low_pass(kept, grad):
    return (grad,)

def back_keep(v):
    return (v, None)

def back_low(kept, grad):
    return (low(grad),)
low.defvjp(low_keep, low_pass)
low_back.defvjp(back_keep, back_low)
EPS = 1e-06

def product(left, right):
    return jnp.dot(left, right, precision=lax.Precision.HIGHEST)

def normalize(values, gain, shift):
    center = values - lax.optimization_barrier(jnp.mean(values, axis=-1, keepdims=True))
    spread = lax.optimization_barrier(jnp.mean(center * center, axis=-1, keepdims=True))
    return center * lax.rsqrt(spread + EPS) * gain + shift

def block(inputs, segment_rows, params):
    query_weight, key_weight, value_weight, query_bias, value_bias, output_weight, output_bias, gain_one, shift_one, inner_weight, inner_bias, down_weight, down_bias, gain_two, shift_two = params
    groups = inputs.shape[0]
    factor = HEAD_DIM ** (-0.5)
    queries = low(low_back(product(inputs, query_weight) + query_bias))
    key_rows = low(low_back(product(inputs, key_weight)))
    values = low(low_back(product(inputs, value_weight) + value_bias))
    shape_heads = (groups, SEQ_LEN, HEADS, HEAD_DIM)
    queries = queries.reshape(shape_heads)
    key_rows = key_rows.reshape(shape_heads)
    values = values.reshape(shape_heads)
    scores = jnp.einsum('gqhd,gkhd->ghqk', queries, key_rows, precision=lax.Precision.HIGHEST) * factor
    allowed = (segment_rows[:, :, None] == segment_rows[:, None, :])[:, None]
    scores = low_back(jnp.where(allowed, scores, -1000000000.0))
    weights = low(jax.nn.softmax(scores, axis=-1))
    context = jnp.einsum('ghqk,gkhd->gqhd', weights, values, precision=lax.Precision.HIGHEST)
    context = low(low_back(context.reshape(groups, SEQ_LEN, D)))
    attention = low_back(product(context, output_weight))
    first_sum = inputs + attention + output_bias
    normed = normalize(first_sum, gain_one, shift_one)
    inner_rows = low_back(product(low(normed), inner_weight) + inner_bias)
    activated = low(jax.nn.gelu(inner_rows, approximate=False))
    mixed = low_back(product(activated, down_weight))
    second_sum = normed + mixed + down_bias
    return normalize(second_sum, gain_two, shift_two)

def reference(tokens, segments, query_weight, key_weight, value_weight, query_bias, value_bias, output_weight, output_bias, gain_one, shift_one, inner_weight, inner_bias, down_weight, down_bias, gain_two, shift_two, cotangent):
    params = tuple((a.astype(jnp.float32) for a in (query_weight, key_weight, value_weight, query_bias, value_bias, output_weight, output_bias, gain_one, shift_one, inner_weight, inner_bias, down_weight, down_bias, gain_two, shift_two)))
    seq_total = TOKENS // SEQ_LEN
    group_size = max((d for d in range(1, seq_total + 1) if seq_total % d == 0 and d * SEQ_LEN <= 4096))
    steps_count = seq_total // group_size
    inputs = tokens.astype(jnp.float32).reshape(steps_count, group_size, SEQ_LEN, D)
    segment_rows = segments.reshape(steps_count, group_size, SEQ_LEN)
    upstream = cotangent.astype(jnp.float32).reshape(steps_count, group_size, SEQ_LEN, D)

    def step(total, item):
        group_in, group_seg, group_up = item
        output, pull = jax.vjp(lambda xin, pin: block(xin, group_seg, pin), group_in, params)
        input_grad, param_grad = pull(group_up)
        total = jax.tree.map(jnp.add, total, param_grad)
        return (total, (output, input_grad))
    zeros = tuple((jnp.zeros_like(a) for a in params))
    grads, (outputs, input_grads) = lax.scan(step, zeros, (inputs, segment_rows, upstream))
    layer_out = outputs.reshape(TOKENS, D).astype(jnp.bfloat16)
    tokens_grad = input_grads.reshape(TOKENS, D)
    return (layer_out, tokens_grad, grads[0], grads[1], grads[2], grads[3], grads[4], grads[5], grads[6], grads[7], grads[8], grads[9], grads[10], grads[11], grads[12], grads[13], grads[14])
```

```python
import functools
import math

import jax
import jax.numpy as jnp
from jax import lax
from jax.experimental import pallas as pl
from jax.experimental.pallas import tpu as pltpu
from jax.sharding import PartitionSpec as P

HEAD_DIM = 64
SEQ_LEN = 512
EPS = 1e-06
MASKED = -1000000000.0
LANES = 8
LOW = jnp.bfloat16
WIDE = jnp.float32
VMEM_LIMIT = 56 * 1024 * 1024

NN = (((1,), (0,)), ((), ()))
NT = (((1,), (1,)), ((), ()))


def dot(left, right, dims):
    return lax.dot_general(left, right, dims, preferred_element_type=WIDE)


def params(**kw):
    return pltpu.CompilerParams(vmem_limit_bytes=VMEM_LIMIT, **kw)


def whole(shape):
    zeros = (0,) * len(shape)
    return pl.BlockSpec(shape, lambda i: zeros)


def rows(block, width):
    return pl.BlockSpec((block, width), lambda i: (i, 0))


def head_mask(width, head):
    lane = lax.broadcasted_iota(jnp.int32, (1, width), 1)
    return (lane >= head * HEAD_DIM) & (lane < (head + 1) * HEAD_DIM)


def same_document(seg_col, seg_row):
    return jnp.where(seg_col == seg_row, jnp.float32(3e38), jnp.float32(MASKED))


def attend_forward(remote, width, x_ref, scol_ref, srow_ref, bias_ref, acc_ref, *rest):
    if remote:
        place_ref, slices, rest = rest[0], rest[1 : 1 + LANES], rest[1 + LANES :]
        qkv_ref, c_ref, l_ref, out_ref, w_ref, wide_ref = rest
        part = width // LANES

        @pl.when(pl.program_id(0) == 0)
        def _():
            here = place_ref[0]
            for m in range(LANES):
                spot = here ^ m
                for t in range(4):
                    at = pl.multiple_of(t * width + spot * part, 8)
                    wide_ref[pl.ds(at, part), :] = slices[m][t * part : (t + 1) * part, :]
            w_ref[...] = wide_ref[...].astype(LOW)
    else:
        w_ref, qkv_ref, c_ref, l_ref, out_ref = rest
    heads = width // HEAD_DIM
    x = x_ref[...]
    qkv = dot(x, w_ref[: 3 * width, :], NT) + bias_ref[...]
    qkv = qkv.astype(LOW)
    qkv_ref[...] = qkv
    queries = qkv[:, :width] * LOW(HEAD_DIM**-0.5)
    keys = qkv[:, width : 2 * width]
    values_t = qkv[:, 2 * width :].T
    limit = same_document(scol_ref[...], srow_ref[0])
    parts = []
    for h in range(heads):
        key_h = jnp.where(head_mask(width, h), keys, LOW(0))
        scores = jnp.minimum(dot(key_h, queries, NT), limit)
        top = jnp.max(scores, axis=0, keepdims=True)
        weights = jnp.exp(scores - top)
        total = jnp.sum(weights, axis=0, keepdims=True)
        l_ref[0, h : h + 1, :] = top + jnp.log(total)
        value_h = values_t[h * HEAD_DIM : (h + 1) * HEAD_DIM, :]
        parts.append(dot(value_h, weights.astype(LOW), NN) / total)
    context = jnp.concatenate(parts, axis=0).T.astype(LOW)
    c_ref[...] = context
    add = dot(context, w_ref[3 * width :, :], NN)
    out_ref[...] = acc_ref[...] + add


def attend_backward(width, own, qkv_ref, c_ref, l_ref, scol_ref, srow_ref, da_ref, w_ref, acc_ref, *rest):
    out_ref = rest[0]
    heads = width // HEAD_DIM
    qkv = qkv_ref[...]
    queries = qkv[:, :width] * LOW(HEAD_DIM**-0.5)
    keys = qkv[:, width : 2 * width]
    values = qkv[:, 2 * width :]
    keys_t = keys.T
    dc = dot(da_ref[...], w_ref[3 * width :, :], NT).astype(LOW)
    prod_t = (dc.astype(WIDE) * c_ref[...].astype(WIDE)).T
    limit = same_document(scol_ref[...], srow_ref[0])
    dq_parts = []
    dk = jnp.zeros((SEQ_LEN, width), WIDE)
    dv = jnp.zeros((SEQ_LEN, width), WIDE)
    for h in range(heads):
        mask = head_mask(width, h)
        key_h = jnp.where(mask, keys, LOW(0))
        query_h = jnp.where(mask, queries, LOW(0))
        value_h = jnp.where(mask, values, LOW(0))
        dc_h = jnp.where(mask, dc, LOW(0))
        scores = jnp.minimum(dot(key_h, queries, NT), limit)
        probs = jnp.exp(scores - l_ref[0, h : h + 1, :])
        dprobs = dot(value_h, dc, NT)
        delta = jnp.sum(prod_t[h * HEAD_DIM : (h + 1) * HEAD_DIM, :], axis=0, keepdims=True)
        dscores = (probs * (dprobs - delta)).astype(LOW)
        dv = dv + dot(probs.astype(LOW), dc_h, NN)
        dk = dk + dot(dscores, query_h, NN)
        dq_parts.append(dot(keys_t[h * HEAD_DIM : (h + 1) * HEAD_DIM, :], dscores, NN))
    dq = jnp.concatenate(dq_parts, axis=0).T * (HEAD_DIM**-0.5)
    dqkv = jnp.concatenate([dq, dk, dv], axis=1).astype(LOW)
    if own:
        rest[1][...] = dqkv
        row_sum = jnp.sum(dqkv.astype(WIDE), axis=0, keepdims=True)
        sum_ref = rest[2]

        @pl.when(pl.program_id(0) == 0)
        def _():
            sum_ref[...] = jnp.zeros_like(sum_ref)

        sum_ref[0:1, :] += row_sum
    out_ref[...] = acc_ref[...] + dot(dqkv, w_ref[: 3 * width, :], NN)


def call_attend_forward(tokens, scol, srow, bias, acc, weight, place, slices):
    count, model = tokens.shape
    width = bias.shape[1] // 3
    seqs = count // SEQ_LEN
    remote = slices is not None
    in_specs = [
        rows(SEQ_LEN, model),
        rows(SEQ_LEN, 1),
        pl.BlockSpec((1, 1, SEQ_LEN), lambda i: (i, 0, 0)),
        whole((1, 3 * width)),
        rows(SEQ_LEN, model),
    ]
    out_specs = [
        rows(SEQ_LEN, 3 * width),
        rows(SEQ_LEN, width),
        pl.BlockSpec((1, 8, SEQ_LEN), lambda i: (i, 0, 0)),
        rows(SEQ_LEN, model),
    ]
    out_shape = [
        jax.ShapeDtypeStruct((count, 3 * width), LOW),
        jax.ShapeDtypeStruct((count, width), LOW),
        jax.ShapeDtypeStruct((seqs, 8, SEQ_LEN), WIDE),
        jax.ShapeDtypeStruct((count, model), WIDE),
    ]
    scratch = []
    if remote:
        in_specs += [pl.BlockSpec(memory_space=pltpu.SMEM)]
        in_specs += [whole(slices[0].shape)] * LANES
        out_specs += [whole((4 * width, model))]
        out_shape += [jax.ShapeDtypeStruct((4 * width, model), LOW)]
        scratch = [pltpu.VMEM((4 * width, model), WIDE)]
        extra = (place, *slices)
    else:
        in_specs += [whole((4 * width, model))]
        extra = (weight,)
    flops = 2 * count * model * width * 4 + 4 * count * SEQ_LEN * width * 4
    return pl.pallas_call(
        functools.partial(attend_forward, remote, width),
        grid=(seqs,),
        in_specs=in_specs,
        out_specs=out_specs,
        out_shape=out_shape,
        scratch_shapes=scratch,
        compiler_params=params(),
        cost_estimate=pl.CostEstimate(
            flops=flops, bytes_accessed=count * model * 12, transcendentals=count * SEQ_LEN * width // HEAD_DIM
        ),
    )(tokens, scol, srow, bias, acc, *extra)


def call_attend_backward(own, qkv, context, logs, scol, srow, da, weight, acc):
    count, model = acc.shape
    width = context.shape[1]
    seqs = count // SEQ_LEN
    in_specs = [
        rows(SEQ_LEN, 3 * width),
        rows(SEQ_LEN, width),
        pl.BlockSpec((1, 8, SEQ_LEN), lambda i: (i, 0, 0)),
        rows(SEQ_LEN, 1),
        pl.BlockSpec((1, 1, SEQ_LEN), lambda i: (i, 0, 0)),
        rows(SEQ_LEN, model),
        whole((4 * width, model)),
        rows(SEQ_LEN, model),
    ]
    out_specs = [rows(SEQ_LEN, model)]
    out_shape = [jax.ShapeDtypeStruct((count, model), WIDE)]
    if own:
        out_specs += [rows(SEQ_LEN, 3 * width), whole((8, 3 * width))]
        out_shape += [
            jax.ShapeDtypeStruct((count, 3 * width), LOW),
            jax.ShapeDtypeStruct((8, 3 * width), WIDE),
        ]
    flops = 2 * count * model * width * 4 + 10 * count * SEQ_LEN * width * 4
    return pl.pallas_call(
        functools.partial(attend_backward, width, own),
        grid=(seqs,),
        in_specs=in_specs,
        out_specs=out_specs,
        out_shape=out_shape,
        compiler_params=params(),
        cost_estimate=pl.CostEstimate(
            flops=flops, bytes_accessed=count * model * 12, transcendentals=count * SEQ_LEN * width // HEAD_DIM
        ),
    )(qkv, context, logs, scol, srow, da, weight, acc)


def gelu_pair(u):
    tail = jnp.exp(u * u * -0.5)
    t = 1.0 / (1.0 + jnp.abs(u) * (0.3275911 * math.sqrt(0.5)))
    poly = 0.5 * 1.061405429
    for c in (-1.453152027, 1.421413741, -0.284496736, 0.254829592):
        poly = poly * t + 0.5 * c
    half = poly * t * tail
    phi = jnp.where(u < 0.0, half, 1.0 - half)
    return u * phi, phi + u * tail * (1.0 / math.sqrt(2.0 * math.pi))


def stats(values):
    mean = jnp.mean(values, axis=1, keepdims=True)
    center = values - mean
    scale = lax.rsqrt(jnp.mean(center * center, axis=1, keepdims=True) + EPS)
    return center * scale, scale


def feed_forward(remote, x_ref, acc_ref, bias_ref, *rest):
    if remote:
        place_ref, slices, rest = rest[0], rest[1 : 1 + LANES], rest[1 + LANES :]
        slope_ref, out_ref, wi_ref, wd_ref = rest
        part = slices[0].shape[0] // 2

        @pl.when(pl.program_id(0) == 0)
        def _():
            here = place_ref[0]
            for m in range(LANES):
                at = pl.multiple_of((here ^ m) * part, part)
                wi_ref[pl.ds(at, part), :] = slices[m][:part, :].astype(LOW)
                wd_ref[pl.ds(at, part), :] = slices[m][part:, :].astype(LOW)

        normed_low = x_ref[...]
    else:
        (obias_ref, gain_ref, shift_ref, wi_ref, wd_ref) = rest[:5]
        slope_ref, out_ref, h1_ref, n1_ref, act_ref = rest[5:]
        h1 = x_ref[...].astype(WIDE) + acc_ref[...] + obias_ref[...]
        h1_ref[...] = h1
        hat, _ = stats(h1)
        normed_low = (hat * gain_ref[...] + shift_ref[...]).astype(LOW)
        n1_ref[...] = normed_low
    hidden = wi_ref.shape[0]
    chunk = 256
    total = None
    for c in range(0, hidden, chunk):
        cols = slice(c, c + chunk)
        u = dot(normed_low, wi_ref[cols, :], NT) + bias_ref[:, cols]
        act, slope = gelu_pair(u)
        act = act.astype(LOW)
        slope_ref[:, cols] = slope.astype(LOW)
        if not remote:
            act_ref[:, cols] = act
        add = dot(act, wd_ref[cols, :], NN)
        total = add if total is None else total + add
    out_ref[...] = total if not remote else acc_ref[...] + total


def call_feed_forward(x, acc, bias, remote, extra, block=512):
    count, model = acc.shape
    hidden = bias.shape[1]
    in_specs = [rows(block, model), rows(block, model), whole((1, hidden))]
    out_specs = [rows(block, hidden), rows(block, model)]
    out_shape = [
        jax.ShapeDtypeStruct((count, hidden), LOW),
        jax.ShapeDtypeStruct((count, model), WIDE),
    ]
    if remote:
        in_specs += [pl.BlockSpec(memory_space=pltpu.SMEM)]
        in_specs += [whole(extra[1].shape)] * LANES
        out_specs += [whole((hidden, model))] * 2
        out_shape += [jax.ShapeDtypeStruct((hidden, model), LOW)] * 2
    else:
        in_specs += [whole((1, model))] * 3 + [whole((hidden, model))] * 2
        out_specs += [rows(block, model), rows(block, model), rows(block, hidden)]
        out_shape += [
            jax.ShapeDtypeStruct((count, model), WIDE),
            jax.ShapeDtypeStruct((count, model), LOW),
            jax.ShapeDtypeStruct((count, hidden), LOW),
        ]
    return pl.pallas_call(
        functools.partial(feed_forward, remote),
        grid=(count // block,),
        in_specs=in_specs,
        out_specs=out_specs,
        out_shape=out_shape,
        compiler_params=params(),
        cost_estimate=pl.CostEstimate(
            flops=4 * count * model * hidden, bytes_accessed=count * model * 14, transcendentals=count * hidden * 2
        ),
    )(x, acc, bias, *extra)


def norm_back(grad, hat, scale, gain):
    d = grad * gain
    first = jnp.mean(d, axis=1, keepdims=True)
    second = jnp.mean(d * hat, axis=1, keepdims=True)
    return scale * (d - first - hat * second)


def column_sum(values):
    return jnp.sum(values, axis=0, keepdims=True)


def middle(groups, h1_ref, m_ref, cot_ref, g1_ref, b1_ref, db_ref, g2_ref, b2_ref, *rest):
    slopes, wis, wds = rest[:groups], rest[groups : 2 * groups], rest[2 * groups : 3 * groups]
    layer_ref, dm_ref, du_ref, dh1_ref, da_ref, sums_ref = rest[3 * groups :]

    @pl.when(pl.program_id(0) == 0)
    def _():
        sums_ref[...] = jnp.zeros_like(sums_ref)

    hat1, scale1 = stats(h1_ref[...])
    normed = hat1 * g1_ref[...] + b1_ref[...]
    hat2, scale2 = stats(normed + m_ref[...] + db_ref[...])
    layer_ref[...] = (hat2 * g2_ref[...] + b2_ref[...]).astype(LOW)
    up = cot_ref[...].astype(WIDE)
    sums_ref[0:1, :] += column_sum(up * hat2)
    sums_ref[1:2, :] += column_sum(up)
    dh2 = norm_back(up, hat2, scale2, g2_ref[...])
    sums_ref[2:3, :] += column_sum(dh2)
    dm = dh2.astype(LOW)
    dm_ref[...] = dm
    dn1 = dh2
    hidden = wis[0].shape[0]
    chunk = 256
    for g in range(groups):
        for c in range(0, hidden, chunk):
            cols = slice(c, c + chunk)
            dact = dot(dm, wds[g][cols, :], NT)
            du = (dact * slopes[g][:, cols].astype(WIDE)).astype(LOW)
            if g == 0:
                du_ref[:, cols] = du
                sums_ref[6:7, cols] += column_sum(du.astype(WIDE))
            dn1 = dn1 + dot(du, wis[g][cols, :], NN)
    sums_ref[3:4, :] += column_sum(dn1 * hat1)
    sums_ref[4:5, :] += column_sum(dn1)
    dh1 = norm_back(dn1, hat1, scale1, g1_ref[...])
    sums_ref[5:6, :] += column_sum(dh1)
    dh1_ref[...] = dh1
    da_ref[...] = dh1.astype(LOW)


def call_middle(h1, mixed, cot, vectors, slopes, wis, wds, block=256):
    count, model = h1.shape
    groups = len(slopes)
    hidden = wis[0].shape[0]
    once = pl.BlockSpec((hidden, model), lambda i: (0, 0), pipeline_mode=pl.Buffered(1))
    in_specs = [rows(block, model)] * 3 + [whole((1, model))] * 5
    in_specs += [rows(block, hidden)] * groups + [once] * (2 * groups)
    out_specs = [
        rows(block, model),
        rows(block, model),
        rows(block, hidden),
        rows(block, model),
        rows(block, model),
        whole((8, model)),
    ]
    out_shape = [
        jax.ShapeDtypeStruct((count, model), LOW),
        jax.ShapeDtypeStruct((count, model), LOW),
        jax.ShapeDtypeStruct((count, hidden), LOW),
        jax.ShapeDtypeStruct((count, model), WIDE),
        jax.ShapeDtypeStruct((count, model), LOW),
        jax.ShapeDtypeStruct((8, model), WIDE),
    ]
    return pl.pallas_call(
        functools.partial(middle, groups),
        grid=(count // block,),
        in_specs=in_specs,
        out_specs=out_specs,
        out_shape=out_shape,
        compiler_params=params(),
        cost_estimate=pl.CostEstimate(
            flops=4 * count * model * hidden * groups, bytes_accessed=count * model * 30, transcendentals=0
        ),
    )(h1, mixed, cot, *vectors, *slopes, *wis, *wds)


def inner_first(left, right):
    return lax.dot_general(left, right, (((0,), (0,)), ((), ())), preferred_element_type=WIDE)


def swap(value, mask, size):
    return lax.ppermute(value, "dp", [(i, i ^ mask) for i in range(size)])


def spread(piece, shift, order, groups, size):
    mine = lax.ppermute(piece, "tensor", [((i + shift) % groups, i) for i in range(groups)])
    first, second = order
    got = {0: mine}
    got[first] = swap(mine, first, size)
    got[second] = swap(mine, second, size)
    got[first ^ second] = swap(got[first], second, size)
    for m in (0, 2, 4, 6):
        got[m ^ 1] = swap(got[m], 1, size)
    return [got[m] for m in range(LANES)]


def per_device(
    groups,
    size,
    tokens,
    segments,
    query_weight,
    key_weight,
    value_weight,
    query_bias,
    value_bias,
    output_weight,
    output_bias,
    gain_one,
    shift_one,
    inner_weight,
    inner_bias,
    down_weight,
    down_bias,
    gain_two,
    shift_two,
    cotangent,
):
    count, model = tokens.shape
    width = query_weight.shape[1]
    hidden = inner_weight.shape[1]
    place = (lax.axis_index("dp") % LANES).astype(jnp.int32)
    place_arg = place.reshape(1)

    qkvo = jnp.concatenate([query_weight.T, key_weight.T, value_weight.T, output_weight], axis=0)
    inner_t = inner_weight.T
    narrow, deep = width // LANES, hidden // LANES
    head_piece = lax.dynamic_slice(
        qkvo.reshape(4, width, model), (0, place * narrow, 0), (4, narrow, model)
    ).reshape(4 * narrow, model).astype(WIDE)
    deep_piece = jnp.concatenate(
        [
            lax.dynamic_slice(inner_t, (place * deep, 0), (deep, model)),
            lax.dynamic_slice(down_weight, (place * deep, 0), (deep, model)),
        ],
        axis=0,
    ).astype(WIDE)
    biases = jnp.concatenate([query_bias, jnp.zeros_like(query_bias), value_bias, inner_bias]).reshape(1, -1)
    bias_of = [biases] + [
        lax.ppermute(biases, "tensor", [((i + j) % groups, i) for i in range(groups)]) for j in range(1, groups)
    ]
    orders = ((2, 4), (4, 2))
    head_slices = [None] + [spread(head_piece, j, orders[j % 2], groups, size) for j in range(1, groups)]
    deep_slices = [None] + [spread(deep_piece, j, orders[(j + 1) % 2], groups, size) for j in range(1, groups)]

    scol = segments.reshape(count, 1)
    srow = segments.reshape(count // SEQ_LEN, 1, SEQ_LEN)
    acc = jnp.zeros((count, model), WIDE)
    saved = []
    for j in range(groups):
        out = call_attend_forward(
            tokens, scol, srow, bias_of[j][:, : 3 * width], acc, qkvo if j == 0 else None, place_arg, head_slices[j]
        )
        qkv, context, logs, acc = out[:4]
        saved.append((qkv, context, logs, qkvo if j == 0 else out[4]))

    row = lambda v: v.reshape(1, -1)
    wis, wds, slopes = [inner_t], [down_weight], []
    slope, mixed, h1, n1, act = call_feed_forward(
        tokens,
        acc,
        biases[:, 3 * width :],
        False,
        (row(output_bias), row(gain_one), row(shift_one), inner_t, down_weight),
    )
    slopes.append(slope)
    for j in range(1, groups):
        slope, mixed, wi, wd = call_feed_forward(
            n1, mixed, bias_of[j][:, 3 * width :], True, (place_arg, *deep_slices[j])
        )
        slopes.append(slope)
        wis.append(wi)
        wds.append(wd)

    vectors = (row(gain_one), row(shift_one), row(down_bias), row(gain_two), row(shift_two))
    layer_out, dm, du, dh1, da, sums = call_middle(h1, mixed, cotangent, vectors, slopes, wis, wds)

    down_part = lax.psum(inner_first(act, dm), "dp")
    inner_part = lax.psum(inner_first(n1, du), "dp")

    acc = dh1
    for j in range(groups):
        qkv, context, logs, weight = saved[j]
        out = call_attend_backward(j == 0, qkv, context, logs, scol, srow, da, weight, acc)
        acc = out[0]
        if j == 0:
            dqkv, qkv_sums = out[1:]
    tokens_grad = acc
    rest = lax.psum(
        (
            inner_first(dqkv, tokens),
            inner_first(saved[0][1], da),
            sums,
            qkv_sums,
        ),
        "dp",
    )
    qkv_grad, output_grad, sums, qkv_sums = rest
    return (
        layer_out,
        tokens_grad,
        qkv_grad[:width].T,
        qkv_grad[width : 2 * width].T,
        qkv_grad[2 * width :].T,
        qkv_sums[0, :width],
        qkv_sums[0, 2 * width :],
        output_grad,
        sums[5],
        sums[3],
        sums[4],
        inner_part,
        sums[6, :hidden],
        down_part,
        sums[2],
        sums[0],
        sums[1],
    )


def solution(mesh):
    whole_rows, columns, lines, split = P("dp", None), P(None, "tensor"), P("tensor", None), P("tensor")
    in_specs = (
        whole_rows, P("dp"), columns, columns, columns, split, split, lines, P(), P(), P(),
        columns, split, lines, P(), P(), P(), whole_rows,
    )
    out_specs = (
        whole_rows, whole_rows, columns, columns, columns, split, split, lines, P(), P(), P(),
        columns, split, lines, P(), P(), P(),
    )
    body = functools.partial(per_device, mesh.shape["tensor"], mesh.shape["dp"])
    return jax.shard_map(body, mesh=mesh, in_specs=in_specs, out_specs=out_specs, check_vma=False)
```

```python
import functools
import math

import jax
import jax.numpy as jnp
from jax import lax
from jax.experimental import pallas as pl
from jax.experimental.pallas import tpu as pltpu
from jax.sharding import PartitionSpec as P

HEAD_DIM = 64
SEQ_LEN = 512
EPS = 1e-06
MASKED = -1000000000.0
LANES = 8
LOW = jnp.bfloat16
WIDE = jnp.float32
VMEM_LIMIT = 56 * 1024 * 1024

NN = (((1,), (0,)), ((), ()))
NT = (((1,), (1,)), ((), ()))


def dot(left, right, dims):
    return lax.dot_general(left, right, dims, preferred_element_type=WIDE)


def params(**kw):
    return pltpu.CompilerParams(vmem_limit_bytes=VMEM_LIMIT, **kw)


def cost(count):
    return pl.CostEstimate(flops=7_500_000 * count, bytes_accessed=8192 * count, transcendentals=0)


def whole(shape):
    zeros = (0,) * len(shape)
    return pl.BlockSpec(shape, lambda i: zeros)


def rows(block, width):
    return pl.BlockSpec((block, width), lambda i: (i, 0))


def head_mask(width, head):
    lane = lax.broadcasted_iota(jnp.int32, (1, width), 1)
    return (lane >= head * HEAD_DIM) & (lane < (head + 1) * HEAD_DIM)


def same_document(seg_col, seg_row):
    return jnp.where(seg_col == seg_row, jnp.float32(3e38), jnp.float32(MASKED))


def attend_forward(remote, width, x_ref, scol_ref, srow_ref, *rest):
    if remote:
        place_ref, slices, rest = rest[0], rest[1 : 1 + LANES], rest[1 + LANES :]
        qkv_ref, c_ref, l_ref, w_ref, wide_ref = rest
        part = width // LANES
        bias = slices[0][4 * part : 4 * part + 1, : 3 * width]

        @pl.when(pl.program_id(0) == 0)
        def _():
            here = place_ref[0]
            for m in range(LANES):
                spot = here ^ m
                for t in range(4):
                    at = pl.multiple_of(t * width + spot * part, 8)
                    wide_ref[pl.ds(at, part), :] = slices[m][t * part : (t + 1) * part, :]
            w_ref[...] = wide_ref[...].astype(LOW)
    else:
        bias_ref, w_ref, qkv_ref, c_ref, l_ref = rest
        bias = bias_ref[...]
    heads = width // HEAD_DIM
    qkv = dot(x_ref[...], w_ref[: 3 * width, :], NT) + bias
    qkv = qkv.astype(LOW)
    qkv_ref[...] = qkv
    queries = qkv[:, :width] * LOW(HEAD_DIM**-0.5)
    keys = qkv[:, width : 2 * width]
    values_t = qkv[:, 2 * width :].T
    limit = same_document(scol_ref[...], srow_ref[0])
    parts = []
    for h in range(heads):
        key_h = jnp.where(head_mask(width, h), keys, LOW(0))
        scores = jnp.minimum(dot(key_h, queries, NT), limit)
        top = jnp.max(scores, axis=0, keepdims=True)
        weights = jnp.exp(scores - top)
        total = jnp.sum(weights, axis=0, keepdims=True)
        l_ref[0, h : h + 1, :] = top + jnp.log(total)
        value_h = values_t[h * HEAD_DIM : (h + 1) * HEAD_DIM, :]
        parts.append(dot(value_h, weights.astype(LOW), NN) / total)
    c_ref[...] = jnp.concatenate(parts, axis=0).T.astype(LOW)


def attend_backward(width, own, qkv_ref, c_ref, l_ref, scol_ref, srow_ref, da_ref, w_ref, dqkv_ref, *rest):
    heads = width // HEAD_DIM
    qkv = qkv_ref[...]
    queries = qkv[:, :width] * LOW(HEAD_DIM**-0.5)
    keys = qkv[:, width : 2 * width]
    values = qkv[:, 2 * width :]
    keys_t = keys.T
    dc = dot(da_ref[...], w_ref[...], NT).astype(LOW)
    prod_t = (dc.astype(WIDE) * c_ref[...].astype(WIDE)).T
    limit = same_document(scol_ref[...], srow_ref[0])
    dq_parts = []
    dk = jnp.zeros((SEQ_LEN, width), WIDE)
    dv = jnp.zeros((SEQ_LEN, width), WIDE)
    for h in range(heads):
        mask = head_mask(width, h)
        key_h = jnp.where(mask, keys, LOW(0))
        query_h = jnp.where(mask, queries, LOW(0))
        value_h = jnp.where(mask, values, LOW(0))
        dc_h = jnp.where(mask, dc, LOW(0))
        scores = jnp.minimum(dot(key_h, queries, NT), limit)
        probs = jnp.exp(scores - l_ref[0, h : h + 1, :])
        dprobs = dot(value_h, dc, NT)
        delta = jnp.sum(prod_t[h * HEAD_DIM : (h + 1) * HEAD_DIM, :], axis=0, keepdims=True)
        dscores = (probs * (dprobs - delta)).astype(LOW)
        dv = dv + dot(probs.astype(LOW), dc_h, NN)
        dk = dk + dot(dscores, query_h, NN)
        dq_parts.append(dot(keys_t[h * HEAD_DIM : (h + 1) * HEAD_DIM, :], dscores, NN))
    dq = jnp.concatenate(dq_parts, axis=0).T * (HEAD_DIM**-0.5)
    dqkv = jnp.concatenate([dq, dk, dv], axis=1).astype(LOW)
    dqkv_ref[...] = dqkv
    if own:
        sum_ref = rest[0]

        @pl.when(pl.program_id(0) == 0)
        def _():
            sum_ref[...] = jnp.zeros_like(sum_ref)

        sum_ref[0:1, : 3 * width] += column_sum(dqkv.astype(WIDE))


def call_attend_forward(width, tokens, scol, srow, bias, weight, place, slices):
    count, model = tokens.shape
    seqs = count // SEQ_LEN
    remote = slices is not None
    in_specs = [
        rows(SEQ_LEN, model),
        rows(SEQ_LEN, 1),
        pl.BlockSpec((1, 1, SEQ_LEN), lambda i: (i, 0, 0)),
    ]
    out_specs = [
        rows(SEQ_LEN, 3 * width),
        rows(SEQ_LEN, width),
        pl.BlockSpec((1, 8, SEQ_LEN), lambda i: (i, 0, 0)),
    ]
    out_shape = [
        jax.ShapeDtypeStruct((count, 3 * width), LOW),
        jax.ShapeDtypeStruct((count, width), LOW),
        jax.ShapeDtypeStruct((seqs, 8, SEQ_LEN), WIDE),
    ]
    scratch = []
    if remote:
        in_specs += [pl.BlockSpec(memory_space=pltpu.SMEM)]
        in_specs += [whole(slices[0].shape)] * LANES
        out_specs += [whole((4 * width, model))]
        out_shape += [jax.ShapeDtypeStruct((4 * width, model), LOW)]
        scratch = [pltpu.VMEM((4 * width, model), WIDE)]
        extra = (place, *slices)
    else:
        in_specs += [whole((1, 3 * width)), whole((4 * width, model))]
        extra = (bias, weight)
    return pl.pallas_call(
        functools.partial(attend_forward, remote, width),
        grid=(seqs,),
        in_specs=in_specs,
        out_specs=out_specs,
        out_shape=out_shape,
        scratch_shapes=scratch,
        compiler_params=params(),
        cost_estimate=cost(count),
    )(tokens, scol, srow, *extra)


def call_attend_backward(own, qkv, context, logs, scol, srow, da, weight):
    count, model = da.shape
    width = context.shape[1]
    seqs = count // SEQ_LEN
    in_specs = [
        rows(SEQ_LEN, 3 * width),
        rows(SEQ_LEN, width),
        pl.BlockSpec((1, 8, SEQ_LEN), lambda i: (i, 0, 0)),
        rows(SEQ_LEN, 1),
        pl.BlockSpec((1, 1, SEQ_LEN), lambda i: (i, 0, 0)),
        rows(SEQ_LEN, model),
        pl.BlockSpec((width, model), lambda i: (3, 0)),
    ]
    out_specs = [rows(SEQ_LEN, 3 * width)]
    out_shape = [jax.ShapeDtypeStruct((count, 3 * width), LOW)]
    if own:
        out_specs += [whole((8, model))]
        out_shape += [jax.ShapeDtypeStruct((8, model), WIDE)]
    return pl.pallas_call(
        functools.partial(attend_backward, width, own),
        grid=(seqs,),
        in_specs=in_specs,
        out_specs=out_specs,
        out_shape=out_shape,
        compiler_params=params(),
        cost_estimate=cost(count),
    )(qkv, context, logs, scol, srow, da, weight)


def input_gradient(groups, dh1_ref, *rest):
    dqkvs, weights, out_ref = rest[:groups], rest[groups : 2 * groups], rest[2 * groups]
    total = dh1_ref[...]
    for dqkv, weight in zip(dqkvs, weights):
        total = total + dot(dqkv[...], weight[: dqkv.shape[1], :], NN)
    out_ref[...] = total


def call_input_gradient(dh1, dqkvs, weights, block=512):
    count, model = dh1.shape
    groups = len(dqkvs)
    wide = dqkvs[0].shape[1]
    once = pl.BlockSpec((wide, model), lambda i: (0, 0), pipeline_mode=pl.Buffered(1))
    return pl.pallas_call(
        functools.partial(input_gradient, groups),
        grid=(count // block,),
        in_specs=[rows(block, model)] + [rows(block, wide)] * groups + [once] * groups,
        out_specs=rows(block, model),
        input_output_aliases={0: 0},
        out_shape=jax.ShapeDtypeStruct((count, model), WIDE),
        compiler_params=params(),
        cost_estimate=cost(count),
    )(dh1, *dqkvs, *weights)


def gelu_pair(u):
    tail = jnp.exp(u * u * -0.5)
    t = 1.0 / (1.0 + jnp.abs(u) * (0.3275911 * math.sqrt(0.5)))
    poly = 0.5 * 1.061405429
    for c in (-1.453152027, 1.421413741, -0.284496736, 0.254829592):
        poly = poly * t + 0.5 * c
    half = poly * t * tail
    phi = jnp.where(u < 0.0, half, 1.0 - half)
    return u * phi, phi + u * tail * (1.0 / math.sqrt(2.0 * math.pi))


def stats(values):
    mean = jnp.mean(values, axis=1, keepdims=True)
    center = values - mean
    scale = lax.rsqrt(jnp.mean(center * center, axis=1, keepdims=True) + EPS)
    return center * scale, scale


def feed_forward(remote, x_ref, *rest):
    if remote:
        acc_ref, rest = rest[0], rest[1:]
        place_ref, slices, rest = rest[0], rest[1 : 1 + LANES], rest[1 + LANES :]
        slope_ref, out_ref, wi_ref, wd_ref = rest
        part = wi_ref.shape[0] // LANES
        bias = slices[0][2 * part : 2 * part + 1, : wi_ref.shape[0]]

        @pl.when(pl.program_id(0) == 0)
        def _():
            here = place_ref[0]
            for m in range(LANES):
                at = pl.multiple_of((here ^ m) * part, part)
                wi_ref[pl.ds(at, part), :] = slices[m][:part, :].astype(LOW)
                wd_ref[pl.ds(at, part), :] = slices[m][part : 2 * part, :].astype(LOW)

        normed_low = x_ref[...]
    else:
        bias_ref, rest = rest[0], rest[1:]
        bias = bias_ref[...]
        (obias_ref, gain_ref, shift_ref, wi_ref, wd_ref) = rest[:5]
        groups = (len(rest) - 10) // 2
        contexts, outs, rest = rest[5 : 5 + groups], rest[5 + groups : 5 + 2 * groups], rest[5 + 2 * groups :]
        slope_ref, out_ref, h1_ref, n1_ref, act_ref = rest
        h1 = x_ref[...].astype(WIDE) + obias_ref[...]
        for context, weight in zip(contexts, outs):
            h1 = h1 + dot(context[...], weight[...], NN)
        h1_ref[...] = h1
        hat, _ = stats(h1)
        normed_low = (hat * gain_ref[...] + shift_ref[...]).astype(LOW)
        n1_ref[...] = normed_low
    hidden = wi_ref.shape[0]
    chunk = 256
    total = None
    for c in range(0, hidden, chunk):
        cols = slice(c, c + chunk)
        u = dot(normed_low, wi_ref[cols, :], NT) + bias[:, cols]
        act, slope = gelu_pair(u)
        act = act.astype(LOW)
        slope_ref[:, cols] = slope.astype(LOW)
        if not remote:
            act_ref[:, cols] = act
        add = dot(act, wd_ref[cols, :], NN)
        total = add if total is None else total + add
    out_ref[...] = total if not remote else acc_ref[...] + total


def call_feed_forward(hidden, x, remote, extra, contexts=(), packs=(), block=512):
    count, model = x.shape
    in_specs = [rows(block, model)]
    out_specs = [rows(block, hidden), rows(block, model)]
    out_shape = [
        jax.ShapeDtypeStruct((count, hidden), LOW),
        jax.ShapeDtypeStruct((count, model), WIDE),
    ]
    if remote:
        in_specs += [rows(block, model), pl.BlockSpec(memory_space=pltpu.SMEM)]
        in_specs += [whole(extra[2].shape)] * LANES
        out_specs += [whole((hidden, model))] * 2
        out_shape += [jax.ShapeDtypeStruct((hidden, model), LOW)] * 2
    else:
        width = contexts[0].shape[1]
        in_specs += [whole((1, hidden))] + [whole((1, model))] * 3 + [whole((hidden, model))] * 2
        in_specs += [rows(block, width)] * len(contexts)
        in_specs += [pl.BlockSpec((width, model), lambda i: (3, 0))] * len(packs)
        out_specs += [rows(block, model), rows(block, model), rows(block, hidden)]
        out_shape += [
            jax.ShapeDtypeStruct((count, model), WIDE),
            jax.ShapeDtypeStruct((count, model), LOW),
            jax.ShapeDtypeStruct((count, hidden), LOW),
        ]
    return pl.pallas_call(
        functools.partial(feed_forward, remote),
        grid=(count // block,),
        in_specs=in_specs,
        out_specs=out_specs,
        out_shape=out_shape,
        input_output_aliases={1: 1} if remote else {},
        compiler_params=params(),
        cost_estimate=cost(count),
    )(x, *extra, *contexts, *packs)


def norm_back(grad, hat, scale, gain):
    d = grad * gain
    first = jnp.mean(d, axis=1, keepdims=True)
    second = jnp.mean(d * hat, axis=1, keepdims=True)
    return scale * (d - first - hat * second)


def column_sum(values):
    return jnp.sum(values, axis=0, keepdims=True)


def back_through(dm, slope, wi_ref, wd_ref, dn1, keep=None):
    chunk = 256
    for c in range(0, wi_ref.shape[0], chunk):
        cols = slice(c, c + chunk)
        dact = dot(dm, wd_ref[cols, :], NT)
        du = (dact * slope[:, cols].astype(WIDE)).astype(LOW)
        if keep is not None:
            keep(cols, du)
        dn1 = dn1 + dot(du, wi_ref[cols, :], NN)
    return dn1


def middle_own(h1_ref, m_ref, cot_ref, g1_ref, b1_ref, db_ref, g2_ref, b2_ref, slope_ref, wi_ref, wd_ref, *outs):
    layer_ref, dm_ref, du_ref, dn1_ref, sums_ref = outs

    @pl.when(pl.program_id(0) == 0)
    def _():
        sums_ref[...] = jnp.zeros_like(sums_ref)

    hat1, _ = stats(h1_ref[...])
    normed = hat1 * g1_ref[...] + b1_ref[...]
    hat2, scale2 = stats(normed + m_ref[...] + db_ref[...])
    layer_ref[...] = (hat2 * g2_ref[...] + b2_ref[...]).astype(LOW)
    up = cot_ref[...].astype(WIDE)
    sums_ref[0:1, :] += column_sum(up * hat2)
    sums_ref[1:2, :] += column_sum(up)
    dh2 = norm_back(up, hat2, scale2, g2_ref[...])
    sums_ref[2:3, :] += column_sum(dh2)
    dm = dh2.astype(LOW)
    dm_ref[...] = dm

    def keep(cols, du):
        du_ref[:, cols] = du
        sums_ref[6:7, cols] += column_sum(du.astype(WIDE))

    dn1_ref[...] = back_through(dm, slope_ref, wi_ref, wd_ref, dh2, keep)


def middle_rest(groups, h1_ref, dn1_ref, dm_ref, g1_ref, old_ref, *rest):
    slopes, wis, wds = rest[:groups], rest[groups : 2 * groups], rest[2 * groups : 3 * groups]
    dh1_ref, da_ref, sums_ref = rest[3 * groups :]

    @pl.when(pl.program_id(0) == 0)
    def _():
        sums_ref[...] = old_ref[...]

    hat1, scale1 = stats(h1_ref[...])
    dm = dm_ref[...]
    dn1 = dn1_ref[...]
    for slope_ref, wi_ref, wd_ref in zip(slopes, wis, wds):
        dn1 = back_through(dm, slope_ref, wi_ref, wd_ref, dn1)
    sums_ref[3:4, :] += column_sum(dn1 * hat1)
    sums_ref[4:5, :] += column_sum(dn1)
    dh1 = norm_back(dn1, hat1, scale1, g1_ref[...])
    sums_ref[5:6, :] += column_sum(dh1)
    dh1_ref[...] = dh1
    da_ref[...] = dh1.astype(LOW)


def call_middle_own(h1, mixed, cot, vectors, slope, wi, wd, block=512):
    count, model = h1.shape
    hidden = wi.shape[0]
    once = pl.BlockSpec((hidden, model), lambda i: (0, 0), pipeline_mode=pl.Buffered(1))
    return pl.pallas_call(
        middle_own,
        grid=(count // block,),
        in_specs=[rows(block, model)] * 3 + [whole((1, model))] * 5 + [rows(block, hidden)] + [once] * 2,
        out_specs=[rows(block, model), rows(block, model), rows(block, hidden), rows(block, model), whole((8, model))],
        out_shape=[
            jax.ShapeDtypeStruct((count, model), LOW),
            jax.ShapeDtypeStruct((count, model), LOW),
            jax.ShapeDtypeStruct((count, hidden), LOW),
            jax.ShapeDtypeStruct((count, model), WIDE),
            jax.ShapeDtypeStruct((8, model), WIDE),
        ],
        input_output_aliases={1: 3},
        compiler_params=params(),
        cost_estimate=cost(count),
    )(h1, mixed, cot, *vectors, slope, wi, wd)


def call_middle_rest(h1, dn1, dm, gain, sums, slopes, wis, wds, block=512):
    count, model = h1.shape
    groups = len(slopes)
    hidden = wis[0].shape[0]
    once = pl.BlockSpec((hidden, model), lambda i: (0, 0), pipeline_mode=pl.Buffered(1))
    return pl.pallas_call(
        functools.partial(middle_rest, groups),
        grid=(count // block,),
        in_specs=[rows(block, model)] * 3
        + [whole((1, model)), whole((8, model))]
        + [rows(block, hidden)] * groups
        + [once] * (2 * groups),
        out_specs=[rows(block, model), rows(block, model), whole((8, model))],
        out_shape=[
            jax.ShapeDtypeStruct((count, model), WIDE),
            jax.ShapeDtypeStruct((count, model), LOW),
            jax.ShapeDtypeStruct((8, model), WIDE),
        ],
        input_output_aliases={1: 0},
        compiler_params=params(),
        cost_estimate=cost(count),
    )(h1, dn1, dm, gain, sums, *slopes, *wis, *wds)


def inner_first(left, right):
    return lax.dot_general(left, right, (((0,), (0,)), ((), ())), preferred_element_type=WIDE)


def assemble(turned, place_ref, *rest):
    pieces, outs = rest[:LANES], rest[LANES:]
    part = pieces[0].shape[0]
    out_ref = rest[-1]
    core, chip = place_ref[0] % 2, place_ref[0] // 2
    for k, piece in enumerate(pieces):
        half = core if k < 4 else 1 - core
        at = pl.multiple_of((half * 4 + (chip ^ (k % 4))) * part, 8)
        out_ref[pl.ds(at, part), :] = piece[...]
    for k in range(turned):
        width = outs[k].shape[1]
        outs[k][...] = out_ref[k * width : (k + 1) * width, :].T
    if turned:
        outs[turned][...] = out_ref[turned * width : (turned + 1) * width, :]


def call_assemble(place, pieces, turned=0):
    part, model = pieces[0].shape
    total = part * LANES
    if turned:
        width = total // (turned + 1)
        shapes = [(model, width)] * turned + [(width, model)]
    else:
        shapes = [(total, model)]
    out = pl.pallas_call(
        functools.partial(assemble, turned),
        grid=(1,),
        in_specs=[pl.BlockSpec(memory_space=pltpu.SMEM)] + [whole((part, model))] * LANES,
        out_specs=[whole(shape) for shape in shapes],
        out_shape=[jax.ShapeDtypeStruct(shape, WIDE) for shape in shapes],
        scratch_shapes=[pltpu.VMEM((total, model), WIDE)] if turned else [],
        compiler_params=params(),
    )(place, *pieces)
    return out


def after(values, *done):
    return lax.optimization_barrier((values, done))[0]


def swap(value, mask, size):
    return lax.ppermute(value, "dp", [(i, i ^ mask) for i in range(size)])


def from_tensor(value, shift, groups):
    return lax.ppermute(value, "tensor", [((i + shift) % groups, i) for i in range(groups)])


class Spread:
    def __init__(self, piece, shift, groups, size):
        self.piece, self.shift, self.groups, self.size = piece, shift, groups, size
        self.got = {}

    def along(self, *done):
        self.got[0] = from_tensor(after(self.piece, *done), self.shift, self.groups)
        return self.got[0]

    def hop(self, m, mask, *done):
        self.got[m ^ mask] = swap(after(self.got[m], *done), mask, self.size)
        return self.got[m ^ mask]

    def pair(self, *done):
        return [self.hop(m, 1, *done) for m in (0, 2, 4, 6)]

    def slices(self):
        return [self.got[m] for m in range(LANES)]


class Total:
    def __init__(self, value, size):
        self.value, self.size = value, size
        self.me = lax.axis_index("dp")
        self.half = value.shape[0] // 2
        self.part = self.half // 4

    def cut(self, value, at, count):
        return lax.dynamic_slice(value, (at, 0), (count, value.shape[1]))

    def pair(self, *done):
        value = after(self.value, *done)
        core = self.me % 2
        self.kept = self.cut(value, core * self.half, self.half)
        self.come = swap(self.cut(value, (1 - core) * self.half, self.half), 1, self.size)
        return self.come

    def scatter(self, *done):
        half = self.kept + after(self.come, *done)
        spot = (self.me // 2) % 4
        parts = [self.cut(half, (spot ^ m) * self.part, self.part) for m in range(4)]
        self.got = [parts[0]] + [swap(parts[m], 2 * m, self.size) for m in (1, 2, 3)]
        return self.got

    def gather(self, *done):
        a, b, c, d = after(self.got, *done)
        total = (a + b) + (c + d)
        mask = LANES
        while mask < self.size:
            total = total + swap(total, mask, self.size)
            mask *= 2
        self.got = [total] + [swap(total, 2 * m, self.size) for m in (1, 2, 3)]
        return self.got

    def share(self, *done):
        self.got = list(after(self.got, *done))
        self.other = [swap(part, 1, self.size) for part in self.got]
        return self.other

    def pieces(self):
        return [*self.got, *self.other]


def per_device(
    groups,
    size,
    tokens,
    segments,
    query_weight,
    key_weight,
    value_weight,
    query_bias,
    value_bias,
    output_weight,
    output_bias,
    gain_one,
    shift_one,
    inner_weight,
    inner_bias,
    down_weight,
    down_bias,
    gain_two,
    shift_two,
    cotangent,
):
    count, model = tokens.shape
    width = query_weight.shape[1]
    hidden = inner_weight.shape[1]
    place = (lax.axis_index("dp") % LANES).astype(jnp.int32)
    place_arg = place.reshape(1)
    others = range(1, groups)
    row = lambda v: v.reshape(1, -1)

    qkvo = jnp.concatenate([query_weight.T, key_weight.T, value_weight.T, output_weight], axis=0)
    inner_t = inner_weight.T
    narrow, deep = width // LANES, hidden // LANES

    def bias_rows(values):
        return jnp.pad(row(values), ((0, 7), (0, model - values.shape[0])))

    head_bias = jnp.concatenate([query_bias, jnp.zeros_like(query_bias), value_bias])
    head_piece = jnp.concatenate(
        [
            lax.dynamic_slice(
                qkvo.reshape(4, width, model), (0, place * narrow, 0), (4, narrow, model)
            ).reshape(4 * narrow, model).astype(WIDE),
            bias_rows(head_bias),
        ],
        axis=0,
    )
    deep_piece = jnp.concatenate(
        [
            lax.dynamic_slice(inner_t, (place * deep, 0), (deep, model)).astype(WIDE),
            lax.dynamic_slice(down_weight, (place * deep, 0), (deep, model)).astype(WIDE),
            bias_rows(inner_bias),
        ],
        axis=0,
    )
    scol = segments.reshape(count, 1)
    srow = segments.reshape(count // SEQ_LEN, 1, SEQ_LEN)

    order = [j for j in others if j % 2] + [j for j in others if j % 2 == 0]
    head_of = [Spread(head_piece, j, groups, size) for j in order]
    deep_of = [Spread(deep_piece, j, groups, size) for j in order]
    saved = {}

    def forward(k, *done):
        if k < 0:
            out = call_attend_forward(
                width, after(tokens, *done), scol, srow, row(head_bias), qkvo, None, None
            )
            saved[0] = (*out, qkvo)
        else:
            slices = after(head_of[k].slices(), *done)
            out = call_attend_forward(width, tokens, scol, srow, None, None, place_arg, slices)
            saved[order[k]] = out
        return out[2]

    a, b, c = head_of
    d, e, f = deep_of
    gate = [a.along()]
    late = c.along(gate)
    gate = [a.hop(0, 2, gate), a.hop(0, 4, gate), a.hop(0, 6, gate), b.along(gate), forward(-1, gate)]
    early = d.along(gate)
    gate = [a.pair(gate), b.hop(0, 2, gate), b.hop(0, 4, gate), late]
    late = e.along(gate)
    gate = [forward(0, gate), b.hop(2, 4, gate), c.hop(0, 2, gate), c.hop(0, 4, gate), early]
    gate = [b.pair(gate), c.hop(4, 2, gate), late]
    late = f.along(gate)
    gate = [forward(1, gate), c.pair(gate), d.hop(0, 2, gate), d.hop(0, 4, gate)]
    gate = [forward(2, gate), d.hop(2, 4, gate), e.hop(0, 2, gate), late]
    slope, mixed, h1, n1, act = call_feed_forward(
        hidden,
        after(tokens, gate),
        False,
        (row(inner_bias), row(output_bias), row(gain_one), row(shift_one), inner_t, down_weight),
        [saved[j][1] for j in range(groups)],
        [saved[j][3] for j in range(groups)],
    )
    slopes, wis, wds = [slope], [inner_t], [down_weight]

    def deep_forward(k, mixed, *done):
        slices = after(deep_of[k].slices(), *done)
        slope, mixed, wi, wd = call_feed_forward(hidden, n1, True, (mixed, place_arg, *slices))
        slopes.append(slope)
        wis.append(wi)
        wds.append(wd)
        return slope, mixed

    gate = [n1, d.pair(gate), e.hop(0, 4, gate), f.hop(0, 2, gate), f.hop(0, 4, gate)]
    begun = [e.hop(4, 2, gate), f.hop(2, 4, gate)]
    slope, mixed = deep_forward(0, mixed, gate)
    gate = [slope, begun]
    gate = [e.pair(gate)]
    begun = [f.pair(gate)]
    slope, mixed = deep_forward(1, mixed, gate)
    gate = [slope, begun]
    slope, mixed = deep_forward(2, mixed, gate)

    vectors = (row(gain_one), row(shift_one), row(down_bias), row(gain_two), row(shift_two))
    layer_out, dm, du, dn1, sums = call_middle_own(h1, mixed, cotangent, vectors, slopes[0], wis[0], wds[0])

    down = Total(inner_first(act, dm), size)
    gate = [down.value]
    inner = Total(inner_first(n1, after(du, gate)), size)
    gate = [down.pair(gate), inner.value]
    gate = [inner.pair(gate)]
    moved = [down.scatter(gate), inner.scatter(gate)]
    dh1, da, sums = call_middle_rest(
        h1, after(dn1, gate), dm, row(gain_one), sums, slopes[1:], wis[1:], wds[1:]
    )
    gate = [moved, sums]

    def backward(j, *done):
        qkv, context, logs, pack = saved[j]
        return call_attend_backward(j == 0, qkv, context, logs, scol, srow, after(da, *done), pack)

    moved = [down.gather(gate)]
    dqkv0, qkv_sums = backward(0, gate)
    sums = jnp.concatenate([sums, qkv_sums], axis=0)
    gate = [dqkv0, moved]
    heads_grad = jnp.concatenate([inner_first(after(dqkv0, gate), tokens), inner_first(saved[0][1], da)], axis=0)
    heads = Total(heads_grad, size)
    gate = [heads_grad]
    dqkvs, packs = [dqkv0], [qkvo]
    for k, j in enumerate(order):
        if k == 0:
            moved = [inner.gather(gate), heads.pair(gate), down.share(gate)]
        elif k == 1:
            moved = [heads.scatter(gate), inner.share(gate)]
        else:
            moved = [heads.gather(gate)]
        mask = 1 << k
        while mask < size:
            sums = after(sums, gate) + swap(after(sums, gate), mask, size)
            mask = mask * 2 if k == len(order) - 1 else size
        (grad,) = backward(j, gate)
        dqkvs.append(grad)
        packs.append(saved[j][3])
        gate = [grad, moved, sums]
    heads.share(gate)
    tokens_grad = call_input_gradient(after(dh1, gate), dqkvs, packs)
    (down_grad,) = call_assemble(place_arg, down.pieces())
    (inner_grad,) = call_assemble(place_arg, inner.pieces())
    query_grad, key_grad, value_grad, output_grad = call_assemble(
        place_arg, after(heads.pieces(), tokens_grad), 3
    )
    return (
        layer_out,
        tokens_grad,
        query_grad,
        key_grad,
        value_grad,
        sums[8, :width],
        sums[8, 2 * width : 3 * width],
        output_grad,
        sums[5],
        sums[3],
        sums[4],
        inner_grad,
        sums[6, :hidden],
        down_grad,
        sums[2],
        sums[0],
        sums[1],
    )


def solution(mesh):
    whole_rows, columns, lines, split = P("dp", None), P(None, "tensor"), P("tensor", None), P("tensor")
    in_specs = (
        whole_rows, P("dp"), columns, columns, columns, split, split, lines, P(), P(), P(),
        columns, split, lines, P(), P(), P(), whole_rows,
    )
    out_specs = (
        whole_rows, whole_rows, columns, columns, columns, split, split, lines, P(), P(), P(),
        columns, split, lines, P(), P(), P(),
    )
    body = functools.partial(per_device, mesh.shape["tensor"], mesh.shape["dp"])
    return jax.shard_map(body, mesh=mesh, in_specs=in_specs, out_specs=out_specs, check_vma=False)
```

```python
import functools
import math

import jax
import jax.numpy as jnp
from jax import lax
from jax.experimental import pallas as pl
from jax.experimental.pallas import tpu as pltpu
from jax.sharding import PartitionSpec as P

HEAD_DIM = 64
SEQ_LEN = 512
EPS = 1e-06
MASKED = -1000000000.0
LANES = 8
LOW = jnp.bfloat16
WIDE = jnp.float32
VMEM_LIMIT = 26 * 1024 * 1024

NN = (((1,), (0,)), ((), ()))
NT = (((1,), (1,)), ((), ()))


def dot(left, right, dims):
    return lax.dot_general(left, right, dims, preferred_element_type=WIDE)


def params(limit=VMEM_LIMIT):
    return pltpu.CompilerParams(vmem_limit_bytes=limit)


def cost(count):
    return pl.CostEstimate(flops=7_500_000 * count, bytes_accessed=8192 * count, transcendentals=0)


def whole(shape):
    zeros = (0,) * len(shape)
    return pl.BlockSpec(shape, lambda i: zeros)


def rows(block, width):
    return pl.BlockSpec((block, width), lambda i: (i, 0))


def head_mask(width, head):
    lane = lax.broadcasted_iota(jnp.int32, (1, width), 1)
    return (lane >= head * HEAD_DIM) & (lane < (head + 1) * HEAD_DIM)


def same_document(seg_col, seg_row):
    return jnp.where(seg_col == seg_row, jnp.float32(3e38), jnp.float32(MASKED))


def attend_forward(remote, width, x_ref, scol_ref, srow_ref, *rest):
    if remote:
        place_ref, slices, rest = rest[0], rest[1 : 1 + LANES], rest[1 + LANES :]
        qkv_ref, c_ref, l_ref, w_ref, wide_ref = rest
        part = width // LANES
        bias = slices[0][4 * part : 4 * part + 1, : 3 * width]

        @pl.when(pl.program_id(0) == 0)
        def _():
            here = place_ref[0]
            for m in range(LANES):
                spot = here ^ m
                for t in range(4):
                    at = pl.multiple_of(t * width + spot * part, 8)
                    wide_ref[pl.ds(at, part), :] = slices[m][t * part : (t + 1) * part, :]
            w_ref[...] = wide_ref[...].astype(LOW)
    else:
        bias_ref, w_ref, qkv_ref, c_ref, l_ref = rest
        bias = bias_ref[...]
    heads = width // HEAD_DIM
    qkv = dot(x_ref[...], w_ref[: 3 * width, :], NT) + bias
    qkv = qkv.astype(LOW)
    qkv_ref[...] = qkv
    queries = qkv[:, :width] * LOW(HEAD_DIM**-0.5)
    keys = qkv[:, width : 2 * width]
    values_t = qkv[:, 2 * width :].T
    limit = same_document(scol_ref[...], srow_ref[0])
    parts = []
    for h in range(heads):
        key_h = jnp.where(head_mask(width, h), keys, LOW(0))
        scores = jnp.minimum(dot(key_h, queries, NT), limit)
        top = jnp.max(scores, axis=0, keepdims=True)
        weights = jnp.exp(scores - top)
        total = jnp.sum(weights, axis=0, keepdims=True)
        l_ref[0, h : h + 1, :] = top + jnp.log(total)
        value_h = values_t[h * HEAD_DIM : (h + 1) * HEAD_DIM, :]
        parts.append(dot(value_h, weights.astype(LOW), NN) / total)
    c_ref[...] = jnp.concatenate(parts, axis=0).T.astype(LOW)


def attend_backward(width, own, qkv_ref, c_ref, l_ref, scol_ref, srow_ref, da_ref, w_ref, dqkv_ref, *rest):
    heads = width // HEAD_DIM
    qkv = qkv_ref[...]
    queries = qkv[:, :width] * LOW(HEAD_DIM**-0.5)
    keys = qkv[:, width : 2 * width]
    values = qkv[:, 2 * width :]
    keys_t = keys.T
    dc = dot(da_ref[...], w_ref[...], NT).astype(LOW)
    prod_t = (dc.astype(WIDE) * c_ref[...].astype(WIDE)).T
    limit = same_document(scol_ref[...], srow_ref[0])
    dq_parts = []
    dk = jnp.zeros((SEQ_LEN, width), WIDE)
    dv = jnp.zeros((SEQ_LEN, width), WIDE)
    for h in range(heads):
        mask = head_mask(width, h)
        key_h = jnp.where(mask, keys, LOW(0))
        query_h = jnp.where(mask, queries, LOW(0))
        value_h = jnp.where(mask, values, LOW(0))
        dc_h = jnp.where(mask, dc, LOW(0))
        scores = jnp.minimum(dot(key_h, queries, NT), limit)
        probs = jnp.exp(scores - l_ref[0, h : h + 1, :])
        dprobs = dot(value_h, dc, NT)
        delta = jnp.sum(prod_t[h * HEAD_DIM : (h + 1) * HEAD_DIM, :], axis=0, keepdims=True)
        dscores = (probs * (dprobs - delta)).astype(LOW)
        dv = dv + dot(probs.astype(LOW), dc_h, NN)
        dk = dk + dot(dscores, query_h, NN)
        dq_parts.append(dot(keys_t[h * HEAD_DIM : (h + 1) * HEAD_DIM, :], dscores, NN))
    dq = jnp.concatenate(dq_parts, axis=0).T * (HEAD_DIM**-0.5)
    dqkv = jnp.concatenate([dq, dk, dv], axis=1).astype(LOW)
    dqkv_ref[...] = dqkv
    if own:
        sum_ref = rest[0]

        @pl.when(pl.program_id(0) == 0)
        def _():
            sum_ref[...] = jnp.zeros_like(sum_ref)

        sum_ref[0:1, : 3 * width] += column_sum(dqkv.astype(WIDE))


def call_attend_forward(width, tokens, scol, srow, bias, weight, place, slices):
    count, model = tokens.shape
    seqs = count // SEQ_LEN
    remote = slices is not None
    in_specs = [
        rows(SEQ_LEN, model),
        rows(SEQ_LEN, 1),
        pl.BlockSpec((1, 1, SEQ_LEN), lambda i: (i, 0, 0)),
    ]
    out_specs = [
        rows(SEQ_LEN, 3 * width),
        rows(SEQ_LEN, width),
        pl.BlockSpec((1, 8, SEQ_LEN), lambda i: (i, 0, 0)),
    ]
    out_shape = [
        jax.ShapeDtypeStruct((count, 3 * width), LOW),
        jax.ShapeDtypeStruct((count, width), LOW),
        jax.ShapeDtypeStruct((seqs, 8, SEQ_LEN), WIDE),
    ]
    scratch = []
    if remote:
        in_specs += [pl.BlockSpec(memory_space=pltpu.SMEM)]
        in_specs += [whole(slices[0].shape)] * LANES
        out_specs += [whole((4 * width, model))]
        out_shape += [jax.ShapeDtypeStruct((4 * width, model), LOW)]
        scratch = [pltpu.VMEM((4 * width, model), WIDE)]
        extra = (place, *slices)
    else:
        in_specs += [whole((1, 3 * width)), whole((4 * width, model))]
        extra = (bias, weight)
    return pl.pallas_call(
        functools.partial(attend_forward, remote, width),
        grid=(seqs,),
        in_specs=in_specs,
        out_specs=out_specs,
        out_shape=out_shape,
        scratch_shapes=scratch,
        compiler_params=params(),
        cost_estimate=cost(count),
    )(tokens, scol, srow, *extra)


def call_attend_backward(own, qkv, context, logs, scol, srow, da, weight):
    count, model = da.shape
    width = context.shape[1]
    seqs = count // SEQ_LEN
    in_specs = [
        rows(SEQ_LEN, 3 * width),
        rows(SEQ_LEN, width),
        pl.BlockSpec((1, 8, SEQ_LEN), lambda i: (i, 0, 0)),
        rows(SEQ_LEN, 1),
        pl.BlockSpec((1, 1, SEQ_LEN), lambda i: (i, 0, 0)),
        rows(SEQ_LEN, model),
        pl.BlockSpec((width, model), lambda i: (3, 0)),
    ]
    out_specs = [rows(SEQ_LEN, 3 * width)]
    out_shape = [jax.ShapeDtypeStruct((count, 3 * width), LOW)]
    if own:
        out_specs += [whole((8, model))]
        out_shape += [jax.ShapeDtypeStruct((8, model), WIDE)]
    return pl.pallas_call(
        functools.partial(attend_backward, width, own),
        grid=(seqs,),
        in_specs=in_specs,
        out_specs=out_specs,
        out_shape=out_shape,
        compiler_params=params(),
        cost_estimate=cost(count),
    )(qkv, context, logs, scol, srow, da, weight)


def input_gradient(groups, dh1_ref, *rest):
    dqkvs, weights, out_ref = rest[:groups], rest[groups : 2 * groups], rest[2 * groups]
    total = dh1_ref[...]
    for dqkv, weight in zip(dqkvs, weights):
        total = total + dot(dqkv[...], weight[: dqkv.shape[1], :], NN)
    out_ref[...] = total


def call_input_gradient(dh1, dqkvs, weights, block=512):
    count, model = dh1.shape
    groups = len(dqkvs)
    wide = dqkvs[0].shape[1]
    once = pl.BlockSpec((wide, model), lambda i: (0, 0), pipeline_mode=pl.Buffered(1))
    return pl.pallas_call(
        functools.partial(input_gradient, groups),
        grid=(count // block,),
        in_specs=[rows(block, model)] + [rows(block, wide)] * groups + [once] * groups,
        out_specs=rows(block, model),
        input_output_aliases={0: 0},
        out_shape=jax.ShapeDtypeStruct((count, model), WIDE),
        compiler_params=params(),
        cost_estimate=cost(count),
    )(dh1, *dqkvs, *weights)


def gelu_pair(u):
    tail = jnp.exp(u * u * -0.5)
    t = 1.0 / (1.0 + jnp.abs(u) * (0.3275911 * math.sqrt(0.5)))
    poly = 0.5 * 1.061405429
    for c in (-1.453152027, 1.421413741, -0.284496736, 0.254829592):
        poly = poly * t + 0.5 * c
    half = poly * t * tail
    phi = jnp.where(u < 0.0, half, 1.0 - half)
    return u * phi, phi + u * tail * (1.0 / math.sqrt(2.0 * math.pi))


def stats(values):
    mean = jnp.mean(values, axis=1, keepdims=True)
    center = values - mean
    scale = lax.rsqrt(jnp.mean(center * center, axis=1, keepdims=True) + EPS)
    return center * scale, scale


def feed_forward(remote, x_ref, *rest):
    if remote:
        acc_ref, rest = rest[0], rest[1:]
        place_ref, slices, rest = rest[0], rest[1 : 1 + LANES], rest[1 + LANES :]
        slope_ref, out_ref, wi_ref, wd_ref = rest
        part = wi_ref.shape[0] // LANES
        bias = slices[0][2 * part : 2 * part + 1, : wi_ref.shape[0]]

        @pl.when(pl.program_id(0) == 0)
        def _():
            here = place_ref[0]
            for m in range(LANES):
                at = pl.multiple_of((here ^ m) * part, part)
                wi_ref[pl.ds(at, part), :] = slices[m][:part, :].astype(LOW)
                wd_ref[pl.ds(at, part), :] = slices[m][part : 2 * part, :].astype(LOW)

        normed_low = x_ref[...]
    else:
        bias_ref, rest = rest[0], rest[1:]
        bias = bias_ref[...]
        (obias_ref, gain_ref, shift_ref, wi_ref, wd_ref) = rest[:5]
        groups = (len(rest) - 10) // 2
        contexts, outs, rest = rest[5 : 5 + groups], rest[5 + groups : 5 + 2 * groups], rest[5 + 2 * groups :]
        slope_ref, out_ref, h1_ref, n1_ref, act_ref = rest
        h1 = x_ref[...].astype(WIDE) + obias_ref[...]
        for context, weight in zip(contexts, outs):
            h1 = h1 + dot(context[...], weight[...], NN)
        h1_ref[...] = h1
        hat, _ = stats(h1)
        normed_low = (hat * gain_ref[...] + shift_ref[...]).astype(LOW)
        n1_ref[...] = normed_low
    hidden = wi_ref.shape[0]
    chunk = 256
    total = None
    for c in range(0, hidden, chunk):
        cols = slice(c, c + chunk)
        u = dot(normed_low, wi_ref[cols, :], NT) + bias[:, cols]
        act, slope = gelu_pair(u)
        act = act.astype(LOW)
        slope_ref[:, cols] = slope.astype(LOW)
        if not remote:
            act_ref[:, cols] = act
        add = dot(act, wd_ref[cols, :], NN)
        total = add if total is None else total + add
    out_ref[...] = total if not remote else acc_ref[...] + total


def call_feed_forward(hidden, x, remote, extra, contexts=(), packs=(), block=512):
    count, model = x.shape
    in_specs = [rows(block, model)]
    out_specs = [rows(block, hidden), rows(block, model)]
    out_shape = [
        jax.ShapeDtypeStruct((count, hidden), LOW),
        jax.ShapeDtypeStruct((count, model), WIDE),
    ]
    if remote:
        in_specs += [rows(block, model), pl.BlockSpec(memory_space=pltpu.SMEM)]
        in_specs += [whole(extra[2].shape)] * LANES
        out_specs += [whole((hidden, model))] * 2
        out_shape += [jax.ShapeDtypeStruct((hidden, model), LOW)] * 2
    else:
        width = contexts[0].shape[1]
        in_specs += [whole((1, hidden))] + [whole((1, model))] * 3 + [whole((hidden, model))] * 2
        in_specs += [rows(block, width)] * len(contexts)
        in_specs += [pl.BlockSpec((width, model), lambda i: (3, 0))] * len(packs)
        out_specs += [rows(block, model), rows(block, model), rows(block, hidden)]
        out_shape += [
            jax.ShapeDtypeStruct((count, model), WIDE),
            jax.ShapeDtypeStruct((count, model), LOW),
            jax.ShapeDtypeStruct((count, hidden), LOW),
        ]
    return pl.pallas_call(
        functools.partial(feed_forward, remote),
        grid=(count // block,),
        in_specs=in_specs,
        out_specs=out_specs,
        out_shape=out_shape,
        input_output_aliases={1: 1} if remote else {},
        compiler_params=params((61 if remote else 26) * 1024 * 1024),
        cost_estimate=cost(count),
    )(x, *extra, *contexts, *packs)


def norm_back(grad, hat, scale, gain):
    d = grad * gain
    first = jnp.mean(d, axis=1, keepdims=True)
    second = jnp.mean(d * hat, axis=1, keepdims=True)
    return scale * (d - first - hat * second)


def column_sum(values):
    return jnp.sum(values, axis=0, keepdims=True)


def back_through(dm, slope, wi_ref, wd_ref, dn1, keep=None):
    chunk = 256
    for c in range(0, wi_ref.shape[0], chunk):
        cols = slice(c, c + chunk)
        dact = dot(dm, wd_ref[cols, :], NT)
        du = (dact * slope[:, cols].astype(WIDE)).astype(LOW)
        if keep is not None:
            keep(cols, du)
        dn1 = dn1 + dot(du, wi_ref[cols, :], NN)
    return dn1


def middle_own(h1_ref, m_ref, cot_ref, g1_ref, b1_ref, db_ref, g2_ref, b2_ref, slope_ref, wi_ref, wd_ref, *outs):
    layer_ref, dm_ref, du_ref, dn1_ref, sums_ref = outs

    @pl.when(pl.program_id(0) == 0)
    def _():
        sums_ref[...] = jnp.zeros_like(sums_ref)

    hat1, _ = stats(h1_ref[...])
    normed = hat1 * g1_ref[...] + b1_ref[...]
    hat2, scale2 = stats(normed + m_ref[...] + db_ref[...])
    layer_ref[...] = (hat2 * g2_ref[...] + b2_ref[...]).astype(LOW)
    up = cot_ref[...].astype(WIDE)
    sums_ref[0:1, :] += column_sum(up * hat2)
    sums_ref[1:2, :] += column_sum(up)
    dh2 = norm_back(up, hat2, scale2, g2_ref[...])
    sums_ref[2:3, :] += column_sum(dh2)
    dm = dh2.astype(LOW)
    dm_ref[...] = dm

    def keep(cols, du):
        du_ref[:, cols] = du
        sums_ref[6:7, cols] += column_sum(du.astype(WIDE))

    dn1_ref[...] = back_through(dm, slope_ref, wi_ref, wd_ref, dh2, keep)


def middle_rest(groups, h1_ref, dn1_ref, dm_ref, g1_ref, old_ref, *rest):
    slopes, wis, wds = rest[:groups], rest[groups : 2 * groups], rest[2 * groups : 3 * groups]
    dh1_ref, da_ref, sums_ref = rest[3 * groups :]

    @pl.when(pl.program_id(0) == 0)
    def _():
        sums_ref[...] = old_ref[...]

    hat1, scale1 = stats(h1_ref[...])
    dm = dm_ref[...]
    dn1 = dn1_ref[...]
    for slope_ref, wi_ref, wd_ref in zip(slopes, wis, wds):
        dn1 = back_through(dm, slope_ref, wi_ref, wd_ref, dn1)
    sums_ref[3:4, :] += column_sum(dn1 * hat1)
    sums_ref[4:5, :] += column_sum(dn1)
    dh1 = norm_back(dn1, hat1, scale1, g1_ref[...])
    sums_ref[5:6, :] += column_sum(dh1)
    dh1_ref[...] = dh1
    da_ref[...] = dh1.astype(LOW)


def call_middle_own(h1, mixed, cot, vectors, slope, wi, wd, block=512):
    count, model = h1.shape
    hidden = wi.shape[0]
    once = pl.BlockSpec((hidden, model), lambda i: (0, 0), pipeline_mode=pl.Buffered(1))
    return pl.pallas_call(
        middle_own,
        grid=(count // block,),
        in_specs=[rows(block, model)] * 3 + [whole((1, model))] * 5 + [rows(block, hidden)] + [once] * 2,
        out_specs=[rows(block, model), rows(block, model), rows(block, hidden), rows(block, model), whole((8, model))],
        out_shape=[
            jax.ShapeDtypeStruct((count, model), LOW),
            jax.ShapeDtypeStruct((count, model), LOW),
            jax.ShapeDtypeStruct((count, hidden), LOW),
            jax.ShapeDtypeStruct((count, model), WIDE),
            jax.ShapeDtypeStruct((8, model), WIDE),
        ],
        input_output_aliases={1: 3},
        compiler_params=params(61 * 1024 * 1024),
        cost_estimate=cost(count),
    )(h1, mixed, cot, *vectors, slope, wi, wd)


def call_middle_rest(h1, dn1, dm, gain, sums, slopes, wis, wds, block=512):
    count, model = h1.shape
    groups = len(slopes)
    hidden = wis[0].shape[0]
    once = pl.BlockSpec((hidden, model), lambda i: (0, 0), pipeline_mode=pl.Buffered(1))
    return pl.pallas_call(
        functools.partial(middle_rest, groups),
        grid=(count // block,),
        in_specs=[rows(block, model)] * 3
        + [whole((1, model)), whole((8, model))]
        + [rows(block, hidden)] * groups
        + [once] * (2 * groups),
        out_specs=[rows(block, model), rows(block, model), whole((8, model))],
        out_shape=[
            jax.ShapeDtypeStruct((count, model), WIDE),
            jax.ShapeDtypeStruct((count, model), LOW),
            jax.ShapeDtypeStruct((8, model), WIDE),
        ],
        input_output_aliases={1: 0},
        compiler_params=params(61 * 1024 * 1024),
        cost_estimate=cost(count),
    )(h1, dn1, dm, gain, sums, *slopes, *wis, *wds)


def inner_first(left, right):
    return lax.dot_general(left, right, (((0,), (0,)), ((), ())), preferred_element_type=WIDE)


def assemble(place_ref, *rest):
    pieces, outs, out_ref = rest[:LANES], rest[LANES:-1], rest[-1]
    part = pieces[0].shape[0]
    core, chip = place_ref[0] % 2, place_ref[0] // 2
    for k, piece in enumerate(pieces):
        half = core if k < 4 else 1 - core
        at = pl.multiple_of((half * 4 + (chip ^ (k % 4))) * part, 8)
        out_ref[pl.ds(at, part), :] = piece[...]
    width = outs[3].shape[0]
    for k in range(4):
        outs[k][...] = out_ref[k * width : (k + 1) * width, :]
    outs[4][...] = out_ref[4 * width : 4 * width + 16, :]


def call_assemble(place, pieces, width):
    part, model = pieces[0].shape
    shapes = [(width, model)] * 4 + [(16, model)]
    return pl.pallas_call(
        assemble,
        grid=(1,),
        in_specs=[pl.BlockSpec(memory_space=pltpu.SMEM)] + [whole((part, model))] * LANES,
        out_specs=[whole(shape) for shape in shapes],
        out_shape=[jax.ShapeDtypeStruct(shape, WIDE) for shape in shapes],
        scratch_shapes=[pltpu.VMEM((part * LANES, model), WIDE)],
        compiler_params=params(),
    )(place, *pieces)


def after(values, *done):
    return lax.optimization_barrier((values, done))[0]


def swap(value, mask, size):
    return lax.ppermute(value, "dp", [(i, i ^ mask) for i in range(size)])


def from_tensor(value, shift, groups):
    return lax.ppermute(value, "tensor", [((i + shift) % groups, i) for i in range(groups)])


class Spread:
    def __init__(self, piece, shift, groups, size):
        self.piece, self.shift, self.groups, self.size = piece, shift, groups, size
        self.got = {}

    def along(self, *done):
        self.got[0] = from_tensor(after(self.piece, *done), self.shift, self.groups)
        return self.got[0]

    def hop(self, m, mask, *done):
        self.got[m ^ mask] = swap(after(self.got[m], *done), mask, self.size)
        return self.got[m ^ mask]

    def slices(self):
        return [self.got[m] for m in range(LANES)]


class Total:
    def __init__(self, value, size):
        self.value, self.size = value, size
        self.me = lax.axis_index("dp")
        self.half = value.shape[0] // 2
        self.part = self.half // 4

    def cut(self, value, at, count):
        return lax.dynamic_slice(value, (at, 0), (count, value.shape[1]))

    def pair(self, *done):
        value = after(self.value, *done)
        core = self.me % 2
        self.kept = self.cut(value, core * self.half, self.half)
        self.come = swap(self.cut(value, (1 - core) * self.half, self.half), 1, self.size)
        return self.come

    def scatter(self, *done):
        half = self.kept + after(self.come, *done)
        spot = (self.me // 2) % 4
        parts = [self.cut(half, (spot ^ m) * self.part, self.part) for m in range(4)]
        self.got = [parts[0]] + [swap(parts[m], 2 * m, self.size) for m in (1, 2, 3)]
        return self.got

    def gather(self, *done):
        a, b, c, d = after(self.got, *done)
        total = (a + b) + (c + d)
        mask = LANES
        while mask < self.size:
            total = total + swap(total, mask, self.size)
            mask *= 2
        self.got = [total] + [swap(total, 2 * m, self.size) for m in (1, 2, 3)]
        return self.got

    def share(self, *done):
        self.got = list(after(self.got, *done))
        self.other = [swap(part, 1, self.size) for part in self.got]
        return self.other

    def pieces(self):
        return [*self.got, *self.other]


def per_device(
    groups,
    size,
    tokens,
    segments,
    query_weight,
    key_weight,
    value_weight,
    query_bias,
    value_bias,
    output_weight,
    output_bias,
    gain_one,
    shift_one,
    inner_weight,
    inner_bias,
    down_weight,
    down_bias,
    gain_two,
    shift_two,
    cotangent,
):
    count, model = tokens.shape
    width = query_weight.shape[1]
    hidden = inner_weight.shape[1]
    place = (lax.axis_index("dp") % LANES).astype(jnp.int32)
    place_arg = place.reshape(1)
    others = range(1, groups)
    row = lambda v: v.reshape(1, -1)

    qkvo = jnp.concatenate([query_weight.T, key_weight.T, value_weight.T, output_weight], axis=0)
    inner_t = inner_weight.T
    narrow, deep = width // LANES, hidden // LANES

    def bias_rows(values):
        return jnp.pad(row(values), ((0, 7), (0, model - values.shape[0])))

    head_bias = jnp.concatenate([query_bias, jnp.zeros_like(query_bias), value_bias])
    head_piece = jnp.concatenate(
        [
            lax.dynamic_slice(
                qkvo.reshape(4, width, model), (0, place * narrow, 0), (4, narrow, model)
            ).reshape(4 * narrow, model).astype(WIDE),
            bias_rows(head_bias),
        ],
        axis=0,
    )
    deep_piece = jnp.concatenate(
        [
            lax.dynamic_slice(inner_t, (place * deep, 0), (deep, model)).astype(WIDE),
            lax.dynamic_slice(down_weight, (place * deep, 0), (deep, model)).astype(WIDE),
            bias_rows(inner_bias),
        ],
        axis=0,
    )
    scol = segments.reshape(count, 1)
    srow = segments.reshape(count // SEQ_LEN, 1, SEQ_LEN)

    order = [j for j in others if j % 2] + [j for j in others if j % 2 == 0]
    head_of = [Spread(head_piece, j, groups, size) for j in order]
    deep_of = [Spread(deep_piece, j, groups, size) for j in order]
    saved = {}

    def forward(k, *done):
        if k < 0:
            out = call_attend_forward(
                width, after(tokens, *done), scol, srow, row(head_bias), qkvo, None, None
            )
            saved[0] = (*out, qkvo)
        else:
            slices = after(head_of[k].slices(), *done)
            out = call_attend_forward(width, tokens, scol, srow, None, None, place_arg, slices)
            saved[order[k]] = out
        return out[2]

    a, b, c = head_of
    d, e, f = deep_of
    gate = [a.along()]
    late = c.along(gate)
    gate = [
        a.hop(0, 2, gate), a.hop(0, 4, gate), a.hop(0, 6, gate), b.along(gate), forward(-1, gate, deep_piece)
    ]
    gate = [a.hop(m, 1, gate) for m in (0, 2, 4, 6)] + [late]
    late = d.along(gate)
    gate = [forward(0, gate), b.hop(0, 2, gate), b.hop(0, 4, gate), b.hop(0, 6, gate), b.hop(0, 1, gate)]
    later = e.along(gate)
    gate = [b.hop(m, 1, gate) for m in (2, 4, 6)] + [late]
    gate = [forward(1, gate), c.hop(0, 2, gate), c.hop(0, 4, gate), c.hop(0, 6, gate), c.hop(0, 1, gate), later]
    begun = [d.hop(0, 2, gate), d.hop(0, 4, gate)]
    gate = [c.hop(m, 1, gate) for m in (2, 4, 6)]
    late = f.along(gate)
    gate = [forward(2, gate), begun, d.hop(0, 1, gate)]
    slope, mixed, h1, n1, act = call_feed_forward(
        hidden,
        after(tokens, gate),
        False,
        (row(inner_bias), row(output_bias), row(gain_one), row(shift_one), inner_t, down_weight),
        [saved[j][1] for j in range(groups)],
        [saved[j][3] for j in range(groups)],
    )
    slopes, wis, wds = [slope], [inner_t], [down_weight]

    def deep_forward(k, mixed, *done):
        slices = after(deep_of[k].slices(), *done)
        slope, mixed, wi, wd = call_feed_forward(hidden, n1, True, (mixed, place_arg, *slices))
        slopes.append(slope)
        wis.append(wi)
        wds.append(wd)
        return slope, mixed

    gate = [n1, d.hop(2, 4, gate), d.hop(2, 1, gate), d.hop(4, 1, gate), e.hop(0, 2, gate), late]
    begun = [e.hop(0, 4, gate), f.hop(0, 2, gate), e.hop(0, 1, gate), e.hop(2, 1, gate)]
    gate = [d.hop(6, 1, gate)]
    slope, mixed = deep_forward(0, mixed, gate)
    gate = [slope, begun]
    begun = [f.hop(0, 4, gate), f.hop(0, 1, gate), f.hop(2, 1, gate)]
    gate = [e.hop(4, 2, gate), e.hop(4, 1, gate), begun]
    begun = [f.hop(4, 2, gate), f.hop(4, 1, gate)]
    gate = [e.hop(6, 1, gate)]
    slope, mixed = deep_forward(1, mixed, gate)
    gate = [slope, begun]
    gate = [f.hop(6, 1, gate)]
    slope, mixed = deep_forward(2, mixed, gate)

    vectors = (row(gain_one), row(shift_one), row(down_bias), row(gain_two), row(shift_two))
    layer_out, dm, du, dn1, sums = call_middle_own(h1, mixed, cotangent, vectors, slopes[0], wis[0], wds[0])

    own = after((inner_first(act, dm), inner_first(n1, du)), dm)
    down_grad, inner_grad = lax.psum(own, "dp")
    dh1, da, sums = call_middle_rest(h1, after(dn1, own), dm, row(gain_one), sums, slopes[1:], wis[1:], wds[1:])

    def backward(j, *done):
        qkv, context, logs, pack = saved[j]
        return call_attend_backward(j == 0, qkv, context, logs, scol, srow, after(da, *done), pack)

    dqkv0, qkv_sums = backward(0)
    parts = [inner_first(dqkv0, tokens), inner_first(saved[0][1], da), sums, qkv_sums]
    used = sum(part.shape[0] for part in parts)
    parts.append(jnp.zeros((-used % (8 * LANES), model), WIDE))
    heads = Total(jnp.concatenate(parts, axis=0), size)
    gate = [heads.value]
    dqkvs, packs = [dqkv0], [qkvo]
    moved = heads.pair(gate)
    for k, j in enumerate(order):
        (grad,) = backward(j, gate)
        dqkvs.append(grad)
        packs.append(saved[j][3])
        gate = [grad]
        if k == 0:
            gate = [grad, moved]
            moved = heads.scatter(gate)
    gate = [gate, moved]
    moved = heads.gather(gate)
    tokens_grad = call_input_gradient(after(dh1, gate), dqkvs, packs)
    heads.share(tokens_grad)
    query_grad, key_grad, value_grad, output_grad, sums = call_assemble(
        place_arg, heads.pieces(), width
    )
    return (
        layer_out,
        tokens_grad,
        query_grad.T,
        key_grad.T,
        value_grad.T,
        sums[8, :width],
        sums[8, 2 * width : 3 * width],
        output_grad,
        sums[5],
        sums[3],
        sums[4],
        inner_grad,
        sums[6, :hidden],
        down_grad,
        sums[2],
        sums[0],
        sums[1],
    )


def solution(mesh):
    whole_rows, columns, lines, split = P("dp", None), P(None, "tensor"), P("tensor", None), P("tensor")
    in_specs = (
        whole_rows, P("dp"), columns, columns, columns, split, split, lines, P(), P(), P(),
        columns, split, lines, P(), P(), P(), whole_rows,
    )
    out_specs = (
        whole_rows, whole_rows, columns, columns, columns, split, split, lines, P(), P(), P(),
        columns, split, lines, P(), P(), P(),
    )
    body = functools.partial(per_device, mesh.shape["tensor"], mesh.shape["dp"])
    return jax.shard_map(body, mesh=mesh, in_specs=in_specs, out_specs=out_specs, check_vma=False)
```

```python
import functools
import math

import jax
import jax.numpy as jnp
from jax import lax
from jax.experimental import pallas as pl
from jax.experimental.pallas import tpu as pltpu
from jax.sharding import PartitionSpec as P

HEAD_DIM = 64
SEQ_LEN = 512
EPS = 1e-06
MASKED = -1000000000.0
LANES = 8
LOW = jnp.bfloat16
WIDE = jnp.float32
VMEM_LIMIT = 26 * 1024 * 1024

NN = (((1,), (0,)), ((), ()))
NT = (((1,), (1,)), ((), ()))


def dot(left, right, dims):
    return lax.dot_general(left, right, dims, preferred_element_type=WIDE)


def params(limit=VMEM_LIMIT):
    return pltpu.CompilerParams(vmem_limit_bytes=limit)


def cost(count):
    return pl.CostEstimate(flops=7_500_000 * count, bytes_accessed=8192 * count, transcendentals=0)


def whole(shape):
    zeros = (0,) * len(shape)
    return pl.BlockSpec(shape, lambda i: zeros)


def rows(block, width):
    return pl.BlockSpec((block, width), lambda i: (i, 0))


def head_mask(width, head):
    lane = lax.broadcasted_iota(jnp.int32, (1, width), 1)
    return (lane >= head * HEAD_DIM) & (lane < (head + 1) * HEAD_DIM)


def same_document(seg_col, seg_row):
    return jnp.where(seg_col == seg_row, jnp.float32(3e38), jnp.float32(MASKED))


def attend_forward(remote, width, x_ref, scol_ref, srow_ref, *rest):
    if remote:
        place_ref, slices, rest = rest[0], rest[1 : 1 + LANES], rest[1 + LANES :]
        qkv_ref, c_ref, l_ref, w_ref, wide_ref = rest
        part = width // LANES
        bias = slices[0][4 * part : 4 * part + 1, : 3 * width]

        @pl.when(pl.program_id(0) == 0)
        def _():
            here = place_ref[0]
            for m in range(LANES):
                spot = here ^ m
                for t in range(4):
                    at = pl.multiple_of(t * width + spot * part, 8)
                    wide_ref[pl.ds(at, part), :] = slices[m][t * part : (t + 1) * part, :]
            w_ref[...] = wide_ref[...].astype(LOW)
    else:
        bias_ref, w_ref, qkv_ref, c_ref, l_ref = rest
        bias = bias_ref[...]
    heads = width // HEAD_DIM
    qkv = dot(x_ref[...], w_ref[: 3 * width, :], NT) + bias
    qkv = qkv.astype(LOW)
    qkv_ref[...] = qkv
    queries = qkv[:, :width] * LOW(HEAD_DIM**-0.5)
    keys = qkv[:, width : 2 * width]
    values_t = qkv[:, 2 * width :].T
    limit = same_document(scol_ref[...], srow_ref[0])
    parts = []
    for h in range(heads):
        key_h = jnp.where(head_mask(width, h), keys, LOW(0))
        scores = jnp.minimum(dot(key_h, queries, NT), limit)
        top = jnp.max(scores, axis=0, keepdims=True)
        weights = jnp.exp(scores - top)
        total = jnp.sum(weights, axis=0, keepdims=True)
        l_ref[0, h : h + 1, :] = top + jnp.log(total)
        value_h = values_t[h * HEAD_DIM : (h + 1) * HEAD_DIM, :]
        parts.append(dot(value_h, weights.astype(LOW), NN) / total)
    c_ref[...] = jnp.concatenate(parts, axis=0).T.astype(LOW)


def attend_backward(width, own, qkv_ref, c_ref, l_ref, scol_ref, srow_ref, da_ref, w_ref, dqkv_ref, *rest):
    heads = width // HEAD_DIM
    qkv = qkv_ref[...]
    queries = qkv[:, :width] * LOW(HEAD_DIM**-0.5)
    keys = qkv[:, width : 2 * width]
    values = qkv[:, 2 * width :]
    keys_t = keys.T
    dc = dot(da_ref[...], w_ref[...], NT).astype(LOW)
    prod_t = (dc.astype(WIDE) * c_ref[...].astype(WIDE)).T
    limit = same_document(scol_ref[...], srow_ref[0])
    dq_parts = []
    dk = jnp.zeros((SEQ_LEN, width), WIDE)
    dv = jnp.zeros((SEQ_LEN, width), WIDE)
    for h in range(heads):
        mask = head_mask(width, h)
        key_h = jnp.where(mask, keys, LOW(0))
        query_h = jnp.where(mask, queries, LOW(0))
        value_h = jnp.where(mask, values, LOW(0))
        dc_h = jnp.where(mask, dc, LOW(0))
        scores = jnp.minimum(dot(key_h, queries, NT), limit)
        probs = jnp.exp(scores - l_ref[0, h : h + 1, :])
        dprobs = dot(value_h, dc, NT)
        delta = jnp.sum(prod_t[h * HEAD_DIM : (h + 1) * HEAD_DIM, :], axis=0, keepdims=True)
        dscores = (probs * (dprobs - delta)).astype(LOW)
        dv = dv + dot(probs.astype(LOW), dc_h, NN)
        dk = dk + dot(dscores, query_h, NN)
        dq_parts.append(dot(keys_t[h * HEAD_DIM : (h + 1) * HEAD_DIM, :], dscores, NN))
    dq = jnp.concatenate(dq_parts, axis=0).T * (HEAD_DIM**-0.5)
    dqkv = jnp.concatenate([dq, dk, dv], axis=1).astype(LOW)
    dqkv_ref[...] = dqkv
    if own:
        sum_ref = rest[0]

        @pl.when(pl.program_id(0) == 0)
        def _():
            sum_ref[...] = jnp.zeros_like(sum_ref)

        sum_ref[0:1, : 3 * width] += column_sum(dqkv.astype(WIDE))


def call_attend_forward(width, tokens, scol, srow, bias, weight, place, slices):
    count, model = tokens.shape
    seqs = count // SEQ_LEN
    remote = slices is not None
    in_specs = [
        rows(SEQ_LEN, model),
        rows(SEQ_LEN, 1),
        pl.BlockSpec((1, 1, SEQ_LEN), lambda i: (i, 0, 0)),
    ]
    out_specs = [
        rows(SEQ_LEN, 3 * width),
        rows(SEQ_LEN, width),
        pl.BlockSpec((1, 8, SEQ_LEN), lambda i: (i, 0, 0)),
    ]
    out_shape = [
        jax.ShapeDtypeStruct((count, 3 * width), LOW),
        jax.ShapeDtypeStruct((count, width), LOW),
        jax.ShapeDtypeStruct((seqs, 8, SEQ_LEN), WIDE),
    ]
    scratch = []
    if remote:
        in_specs += [pl.BlockSpec(memory_space=pltpu.SMEM)]
        in_specs += [whole(slices[0].shape)] * LANES
        out_specs += [whole((4 * width, model))]
        out_shape += [jax.ShapeDtypeStruct((4 * width, model), LOW)]
        scratch = [pltpu.VMEM((4 * width, model), WIDE)]
        extra = (place, *slices)
    else:
        in_specs += [whole((1, 3 * width)), whole((4 * width, model))]
        extra = (bias, weight)
    return pl.pallas_call(
        functools.partial(attend_forward, remote, width),
        grid=(seqs,),
        in_specs=in_specs,
        out_specs=out_specs,
        out_shape=out_shape,
        scratch_shapes=scratch,
        compiler_params=params(),
        cost_estimate=cost(count),
    )(tokens, scol, srow, *extra)


def call_attend_backward(own, qkv, context, logs, scol, srow, da, weight):
    count, model = da.shape
    width = context.shape[1]
    seqs = count // SEQ_LEN
    in_specs = [
        rows(SEQ_LEN, 3 * width),
        rows(SEQ_LEN, width),
        pl.BlockSpec((1, 8, SEQ_LEN), lambda i: (i, 0, 0)),
        rows(SEQ_LEN, 1),
        pl.BlockSpec((1, 1, SEQ_LEN), lambda i: (i, 0, 0)),
        rows(SEQ_LEN, model),
        pl.BlockSpec((width, model), lambda i: (3, 0)),
    ]
    out_specs = [rows(SEQ_LEN, 3 * width)]
    out_shape = [jax.ShapeDtypeStruct((count, 3 * width), LOW)]
    if own:
        out_specs += [whole((8, model))]
        out_shape += [jax.ShapeDtypeStruct((8, model), WIDE)]
    return pl.pallas_call(
        functools.partial(attend_backward, width, own),
        grid=(seqs,),
        in_specs=in_specs,
        out_specs=out_specs,
        out_shape=out_shape,
        compiler_params=params(),
        cost_estimate=cost(count),
    )(qkv, context, logs, scol, srow, da, weight)


def input_gradient(groups, dh1_ref, *rest):
    dqkvs, weights, out_ref = rest[:groups], rest[groups : 2 * groups], rest[2 * groups]
    total = dh1_ref[...]
    for dqkv, weight in zip(dqkvs, weights):
        total = total + dot(dqkv[...], weight[: dqkv.shape[1], :], NN)
    out_ref[...] = total


def call_input_gradient(dh1, dqkvs, weights, block=512):
    count, model = dh1.shape
    groups = len(dqkvs)
    wide = dqkvs[0].shape[1]
    once = pl.BlockSpec((wide, model), lambda i: (0, 0), pipeline_mode=pl.Buffered(1))
    return pl.pallas_call(
        functools.partial(input_gradient, groups),
        grid=(count // block,),
        in_specs=[rows(block, model)] + [rows(block, wide)] * groups + [once] * groups,
        out_specs=rows(block, model),
        input_output_aliases={0: 0},
        out_shape=jax.ShapeDtypeStruct((count, model), WIDE),
        compiler_params=params(),
        cost_estimate=cost(count),
    )(dh1, *dqkvs, *weights)


def gelu_pair(u):
    tail = jnp.exp(u * u * -0.5)
    t = 1.0 / (1.0 + jnp.abs(u) * (0.3275911 * math.sqrt(0.5)))
    poly = 0.5 * 1.061405429
    for c in (-1.453152027, 1.421413741, -0.284496736, 0.254829592):
        poly = poly * t + 0.5 * c
    half = poly * t * tail
    phi = jnp.where(u < 0.0, half, 1.0 - half)
    return u * phi, phi + u * tail * (1.0 / math.sqrt(2.0 * math.pi))


def stats(values):
    mean = jnp.mean(values, axis=1, keepdims=True)
    center = values - mean
    scale = lax.rsqrt(jnp.mean(center * center, axis=1, keepdims=True) + EPS)
    return center * scale, scale


def feed_forward(remote, x_ref, *rest):
    if remote:
        acc_ref, rest = rest[0], rest[1:]
        place_ref, slices, rest = rest[0], rest[1 : 1 + LANES], rest[1 + LANES :]
        slope_ref, out_ref, wi_ref, wd_ref = rest
        part = wi_ref.shape[0] // LANES
        bias = slices[0][2 * part : 2 * part + 1, : wi_ref.shape[0]]

        @pl.when(pl.program_id(0) == 0)
        def _():
            here = place_ref[0]
            for m in range(LANES):
                at = pl.multiple_of((here ^ m) * part, part)
                wi_ref[pl.ds(at, part), :] = slices[m][:part, :].astype(LOW)
                wd_ref[pl.ds(at, part), :] = slices[m][part : 2 * part, :].astype(LOW)

        normed_low = x_ref[...]
    else:
        bias_ref, rest = rest[0], rest[1:]
        bias = bias_ref[...]
        (obias_ref, gain_ref, shift_ref, wi_ref, wd_ref) = rest[:5]
        groups = (len(rest) - 10) // 2
        contexts, outs, rest = rest[5 : 5 + groups], rest[5 + groups : 5 + 2 * groups], rest[5 + 2 * groups :]
        slope_ref, out_ref, h1_ref, n1_ref, act_ref = rest
        h1 = x_ref[...].astype(WIDE) + obias_ref[...]
        for context, weight in zip(contexts, outs):
            h1 = h1 + dot(context[...], weight[...], NN)
        h1_ref[...] = h1
        hat, _ = stats(h1)
        normed_low = (hat * gain_ref[...] + shift_ref[...]).astype(LOW)
        n1_ref[...] = normed_low
    hidden = wi_ref.shape[0]
    chunk = 768
    total = None
    for c in range(0, hidden, chunk):
        cols = slice(c, c + chunk)
        u = dot(normed_low, wi_ref[cols, :], NT) + bias[:, cols]
        act, slope = gelu_pair(u)
        act = act.astype(LOW)
        slope_ref[:, cols] = slope.astype(LOW)
        if not remote:
            act_ref[:, cols] = act
        add = dot(act, wd_ref[cols, :], NN)
        total = add if total is None else total + add
    out_ref[...] = total if not remote else acc_ref[...] + total


def call_feed_forward(hidden, x, remote, extra, contexts=(), packs=(), block=512):
    count, model = x.shape
    in_specs = [rows(block, model)]
    out_specs = [rows(block, hidden), rows(block, model)]
    out_shape = [
        jax.ShapeDtypeStruct((count, hidden), LOW),
        jax.ShapeDtypeStruct((count, model), WIDE),
    ]
    if remote:
        in_specs += [rows(block, model), pl.BlockSpec(memory_space=pltpu.SMEM)]
        in_specs += [whole(extra[2].shape)] * LANES
        out_specs += [whole((hidden, model))] * 2
        out_shape += [jax.ShapeDtypeStruct((hidden, model), LOW)] * 2
    else:
        width = contexts[0].shape[1]
        in_specs += [whole((1, hidden))] + [whole((1, model))] * 3 + [whole((hidden, model))] * 2
        in_specs += [rows(block, width)] * len(contexts)
        in_specs += [pl.BlockSpec((width, model), lambda i: (3, 0))] * len(packs)
        out_specs += [rows(block, model), rows(block, model), rows(block, hidden)]
        out_shape += [
            jax.ShapeDtypeStruct((count, model), WIDE),
            jax.ShapeDtypeStruct((count, model), LOW),
            jax.ShapeDtypeStruct((count, hidden), LOW),
        ]
    return pl.pallas_call(
        functools.partial(feed_forward, remote),
        grid=(count // block,),
        in_specs=in_specs,
        out_specs=out_specs,
        out_shape=out_shape,
        input_output_aliases={1: 1} if remote else {},
        compiler_params=params((61 if remote else 26) * 1024 * 1024),
        cost_estimate=cost(count),
    )(x, *extra, *contexts, *packs)


def norm_back(grad, hat, scale, gain):
    d = grad * gain
    first = jnp.mean(d, axis=1, keepdims=True)
    second = jnp.mean(d * hat, axis=1, keepdims=True)
    return scale * (d - first - hat * second)


def column_sum(values):
    return jnp.sum(values, axis=0, keepdims=True)


def back_through(dm, slope, wi_ref, wd_ref, dn1, keep=None):
    chunk = 768
    for c in range(0, wi_ref.shape[0], chunk):
        cols = slice(c, c + chunk)
        dact = dot(dm, wd_ref[cols, :], NT)
        du = (dact * slope[:, cols].astype(WIDE)).astype(LOW)
        if keep is not None:
            keep(cols, du)
        dn1 = dn1 + dot(du, wi_ref[cols, :], NN)
    return dn1


def middle_own(h1_ref, m_ref, cot_ref, g1_ref, b1_ref, db_ref, g2_ref, b2_ref, slope_ref, wi_ref, wd_ref, act_ref, n1_ref, *outs):
    layer_ref, dm_ref, dn1_ref, sums_ref, down_ref, inner_ref = outs

    @pl.when(pl.program_id(0) == 0)
    def _():
        sums_ref[...] = jnp.zeros_like(sums_ref)
        down_ref[...] = jnp.zeros_like(down_ref)
        inner_ref[...] = jnp.zeros_like(inner_ref)

    hat1, _ = stats(h1_ref[...])
    normed = hat1 * g1_ref[...] + b1_ref[...]
    hat2, scale2 = stats(normed + m_ref[...] + db_ref[...])
    layer_ref[...] = (hat2 * g2_ref[...] + b2_ref[...]).astype(LOW)
    up = cot_ref[...].astype(WIDE)
    sums_ref[0:1, :] += column_sum(up * hat2)
    sums_ref[1:2, :] += column_sum(up)
    dh2 = norm_back(up, hat2, scale2, g2_ref[...])
    sums_ref[2:3, :] += column_sum(dh2)
    dm = dh2.astype(LOW)
    dm_ref[...] = dm
    down_ref[...] += inner_first(act_ref[...], dm)

    def keep(cols, du):
        inner_ref[:, cols] += inner_first(n1_ref[...], du)
        sums_ref[6:7, cols] += column_sum(du.astype(WIDE))

    dn1_ref[...] = back_through(dm, slope_ref, wi_ref, wd_ref, dh2, keep)


def middle_rest(groups, h1_ref, dn1_ref, dm_ref, g1_ref, old_ref, *rest):
    slopes, wis, wds = rest[:groups], rest[groups : 2 * groups], rest[2 * groups : 3 * groups]
    dh1_ref, da_ref, sums_ref = rest[3 * groups :]

    @pl.when(pl.program_id(0) == 0)
    def _():
        sums_ref[...] = old_ref[...]

    hat1, scale1 = stats(h1_ref[...])
    dm = dm_ref[...]
    dn1 = dn1_ref[...]
    for slope_ref, wi_ref, wd_ref in zip(slopes, wis, wds):
        dn1 = back_through(dm, slope_ref, wi_ref, wd_ref, dn1)
    sums_ref[3:4, :] += column_sum(dn1 * hat1)
    sums_ref[4:5, :] += column_sum(dn1)
    dh1 = norm_back(dn1, hat1, scale1, g1_ref[...])
    sums_ref[5:6, :] += column_sum(dh1)
    dh1_ref[...] = dh1
    da_ref[...] = dh1.astype(LOW)


def call_middle_own(h1, mixed, cot, vectors, slope, wi, wd, act, n1, block=512):
    count, model = h1.shape
    hidden = wi.shape[0]
    once = pl.BlockSpec((hidden, model), lambda i: (0, 0), pipeline_mode=pl.Buffered(1))
    return pl.pallas_call(
        middle_own,
        grid=(count // block,),
        in_specs=[rows(block, model)] * 3 + [whole((1, model))] * 5 + [rows(block, hidden)] + [once] * 2
        + [rows(block, hidden), rows(block, model)],
        out_specs=[rows(block, model)] * 3 + [whole((8, model)), whole((hidden, model)), whole((model, hidden))],
        out_shape=[
            jax.ShapeDtypeStruct((count, model), LOW),
            jax.ShapeDtypeStruct((count, model), LOW),
            jax.ShapeDtypeStruct((count, model), WIDE),
            jax.ShapeDtypeStruct((8, model), WIDE),
            jax.ShapeDtypeStruct((hidden, model), WIDE),
            jax.ShapeDtypeStruct((model, hidden), WIDE),
        ],
        input_output_aliases={1: 2},
        compiler_params=params(61 * 1024 * 1024),
        cost_estimate=cost(count),
    )(h1, mixed, cot, *vectors, slope, wi, wd, act, n1)


def call_middle_rest(h1, dn1, dm, gain, sums, slopes, wis, wds, block=512):
    count, model = h1.shape
    groups = len(slopes)
    hidden = wis[0].shape[0]
    once = pl.BlockSpec((hidden, model), lambda i: (0, 0), pipeline_mode=pl.Buffered(1))
    return pl.pallas_call(
        functools.partial(middle_rest, groups),
        grid=(count // block,),
        in_specs=[rows(block, model)] * 3
        + [whole((1, model)), whole((8, model))]
        + [rows(block, hidden)] * groups
        + [once] * (2 * groups),
        out_specs=[rows(block, model), rows(block, model), whole((8, model))],
        out_shape=[
            jax.ShapeDtypeStruct((count, model), WIDE),
            jax.ShapeDtypeStruct((count, model), LOW),
            jax.ShapeDtypeStruct((8, model), WIDE),
        ],
        input_output_aliases={1: 0},
        compiler_params=params(61 * 1024 * 1024),
        cost_estimate=cost(count),
    )(h1, dn1, dm, gain, sums, *slopes, *wis, *wds)


def inner_first(left, right):
    return lax.dot_general(left, right, (((0,), (0,)), ((), ())), preferred_element_type=WIDE)


def assemble(place_ref, *rest):
    pieces, outs, out_ref = rest[:LANES], rest[LANES:-1], rest[-1]
    part = pieces[0].shape[0]
    core, chip = place_ref[0] % 2, place_ref[0] // 2
    for k, piece in enumerate(pieces):
        half = core if k < 4 else 1 - core
        at = pl.multiple_of((half * 4 + (chip ^ (k % 4))) * part, 8)
        out_ref[pl.ds(at, part), :] = piece[...]
    width = outs[3].shape[0]
    for k in range(4):
        outs[k][...] = out_ref[k * width : (k + 1) * width, :]
    outs[4][...] = out_ref[4 * width : 4 * width + 16, :]


def call_assemble(place, pieces, width):
    part, model = pieces[0].shape
    shapes = [(width, model)] * 4 + [(16, model)]
    return pl.pallas_call(
        assemble,
        grid=(1,),
        in_specs=[pl.BlockSpec(memory_space=pltpu.SMEM)] + [whole((part, model))] * LANES,
        out_specs=[whole(shape) for shape in shapes],
        out_shape=[jax.ShapeDtypeStruct(shape, WIDE) for shape in shapes],
        scratch_shapes=[pltpu.VMEM((part * LANES, model), WIDE)],
        compiler_params=params(),
    )(place, *pieces)


def after(values, *done):
    return lax.optimization_barrier((values, done))[0]


def swap(value, mask, size):
    return lax.ppermute(value, "dp", [(i, i ^ mask) for i in range(size)])


def from_tensor(value, shift, groups):
    return lax.ppermute(value, "tensor", [((i + shift) % groups, i) for i in range(groups)])


class Spread:
    def __init__(self, piece, shift, groups, size):
        self.piece, self.shift, self.groups, self.size = piece, shift, groups, size
        self.got = {}

    def along(self, *done):
        self.got[0] = from_tensor(after(self.piece, *done), self.shift, self.groups)
        return self.got[0]

    def hop(self, m, mask, *done):
        self.got[m ^ mask] = swap(after(self.got[m], *done), mask, self.size)
        return self.got[m ^ mask]

    def slices(self):
        return [self.got[m] for m in range(LANES)]


class Total:
    def __init__(self, value, size):
        self.value, self.size = value, size
        self.me = lax.axis_index("dp")
        self.half = value.shape[0] // 2
        self.part = self.half // 4

    def cut(self, value, at, count):
        return lax.dynamic_slice(value, (at, 0), (count, value.shape[1]))

    def pair(self, *done):
        value = after(self.value, *done)
        core = self.me % 2
        self.kept = self.cut(value, core * self.half, self.half)
        self.come = swap(self.cut(value, (1 - core) * self.half, self.half), 1, self.size)
        return self.come

    def scatter(self, *done):
        half = self.kept + after(self.come, *done)
        spot = (self.me // 2) % 4
        parts = [self.cut(half, (spot ^ m) * self.part, self.part) for m in range(4)]
        self.got = [parts[0]] + [swap(parts[m], 2 * m, self.size) for m in (1, 2, 3)]
        return self.got

    def gather(self, *done):
        a, b, c, d = after(self.got, *done)
        total = (a + b) + (c + d)
        mask = LANES
        while mask < self.size:
            total = total + swap(total, mask, self.size)
            mask *= 2
        self.got = [total] + [swap(total, 2 * m, self.size) for m in (1, 2, 3)]
        return self.got

    def share(self, *done):
        self.got = list(after(self.got, *done))
        self.other = [swap(part, 1, self.size) for part in self.got]
        return self.other

    def pieces(self):
        return [*self.got, *self.other]


def per_device(
    groups,
    size,
    tokens,
    segments,
    query_weight,
    key_weight,
    value_weight,
    query_bias,
    value_bias,
    output_weight,
    output_bias,
    gain_one,
    shift_one,
    inner_weight,
    inner_bias,
    down_weight,
    down_bias,
    gain_two,
    shift_two,
    cotangent,
):
    count, model = tokens.shape
    width = query_weight.shape[1]
    hidden = inner_weight.shape[1]
    place = (lax.axis_index("dp") % LANES).astype(jnp.int32)
    place_arg = place.reshape(1)
    others = range(1, groups)
    row = lambda v: v.reshape(1, -1)

    qkvo = jnp.concatenate([query_weight.T, key_weight.T, value_weight.T, output_weight], axis=0)
    inner_t = inner_weight.T
    narrow, deep = width // LANES, hidden // LANES

    def bias_rows(values):
        return jnp.pad(row(values), ((0, 7), (0, model - values.shape[0])))

    head_bias = jnp.concatenate([query_bias, jnp.zeros_like(query_bias), value_bias])
    head_piece = jnp.concatenate(
        [
            lax.dynamic_slice(
                qkvo.reshape(4, width, model), (0, place * narrow, 0), (4, narrow, model)
            ).reshape(4 * narrow, model).astype(WIDE),
            bias_rows(head_bias),
        ],
        axis=0,
    )
    deep_piece = jnp.concatenate(
        [
            lax.dynamic_slice(inner_t, (place * deep, 0), (deep, model)).astype(WIDE),
            lax.dynamic_slice(down_weight, (place * deep, 0), (deep, model)).astype(WIDE),
            bias_rows(inner_bias),
        ],
        axis=0,
    )
    scol = segments.reshape(count, 1)
    srow = segments.reshape(count // SEQ_LEN, 1, SEQ_LEN)

    order = [j for j in others if j % 2] + [j for j in others if j % 2 == 0]
    head_of = [Spread(head_piece, j, groups, size) for j in order]
    deep_of = [Spread(deep_piece, j, groups, size) for j in order]
    saved = {}

    def forward(k, *done):
        if k < 0:
            out = call_attend_forward(
                width, after(tokens, *done), scol, srow, row(head_bias), qkvo, None, None
            )
            saved[0] = (*out, qkvo)
        else:
            slices = after(head_of[k].slices(), *done)
            out = call_attend_forward(width, tokens, scol, srow, None, None, place_arg, slices)
            saved[order[k]] = out
        return out[2]

    a, b, c = head_of
    d, e, f = deep_of
    gate = [a.along()]
    late = c.along(gate)
    gate = [
        a.hop(0, 2, gate), a.hop(0, 4, gate), a.hop(0, 6, gate), b.along(gate), forward(-1, gate, deep_piece)
    ]
    gate = [a.hop(m, 1, gate) for m in (0, 2, 4, 6)] + [late]
    late = d.along(gate)
    gate = [forward(0, gate), b.hop(0, 2, gate), b.hop(0, 4, gate), b.hop(0, 6, gate), b.hop(0, 1, gate)]
    later = e.along(gate)
    gate = [b.hop(m, 1, gate) for m in (2, 4, 6)] + [late]
    gate = [forward(1, gate), c.hop(0, 2, gate), c.hop(0, 4, gate), c.hop(0, 6, gate), c.hop(0, 1, gate), later]
    begun = [d.hop(0, 2, gate), d.hop(0, 4, gate)]
    gate = [c.hop(m, 1, gate) for m in (2, 4, 6)]
    late = [f.along(gate), e.hop(0, 2, gate)]
    gate = [forward(2, gate), begun, d.hop(0, 1, gate)]
    slope, mixed, h1, n1, act = call_feed_forward(
        hidden,
        after(tokens, gate),
        False,
        (row(inner_bias), row(output_bias), row(gain_one), row(shift_one), inner_t, down_weight),
        [saved[j][1] for j in range(groups)],
        [saved[j][3] for j in range(groups)],
    )
    slopes, wis, wds = [slope], [inner_t], [down_weight]

    def deep_forward(k, mixed, *done):
        slices = after(deep_of[k].slices(), *done)
        slope, mixed, wi, wd = call_feed_forward(hidden, n1, True, (mixed, place_arg, *slices))
        slopes.append(slope)
        wis.append(wi)
        wds.append(wd)
        return slope, mixed

    gate = [n1, d.hop(2, 4, gate), d.hop(2, 1, gate), e.hop(0, 4, gate), late]
    begun = [f.hop(0, 4, gate)]
    late = e.hop(4, 2, gate)
    gate = [d.hop(4, 1, gate), d.hop(6, 1, gate)]
    begun += [e.hop(0, 1, gate), e.hop(2, 1, gate)]
    queued = f.hop(0, 2, gate)
    slope, mixed = deep_forward(0, mixed, gate)
    gate = [slope, begun, late]
    begun = [f.hop(4, 2, gate), f.hop(0, 1, gate), queued]
    gate = [e.hop(4, 1, gate), e.hop(6, 1, gate)]
    begun += [f.hop(4, 1, gate)]
    slope, mixed = deep_forward(1, mixed, gate)
    gate = [slope, begun]
    gate = [f.hop(2, 1, gate), f.hop(6, 1, gate)]
    slope, mixed = deep_forward(2, mixed, gate)

    vectors = (row(gain_one), row(shift_one), row(down_bias), row(gain_two), row(shift_two))
    layer_out, dm, dn1, sums, *own = call_middle_own(
        h1, mixed, cotangent, vectors, slopes[0], wis[0], wds[0], act, n1
    )

    own = after(tuple(own), dm)
    down_grad, inner_grad = lax.psum(own, "dp")
    dh1, da, sums = call_middle_rest(h1, after(dn1, own), dm, row(gain_one), sums, slopes[1:], wis[1:], wds[1:])

    def backward(j, *done):
        qkv, context, logs, pack = saved[j]
        return call_attend_backward(j == 0, qkv, context, logs, scol, srow, after(da, *done), pack)

    dqkv0, qkv_sums = backward(0)
    parts = [inner_first(dqkv0, tokens), inner_first(saved[0][1], da), sums, qkv_sums]
    used = sum(part.shape[0] for part in parts)
    parts.append(jnp.zeros((-used % (8 * LANES), model), WIDE))
    heads = Total(jnp.concatenate(parts, axis=0), size)
    gate = [heads.value]
    dqkvs, packs = [dqkv0], [qkvo]
    moved = heads.pair(gate)
    for k, j in enumerate(order):
        (grad,) = backward(j, gate)
        dqkvs.append(grad)
        packs.append(saved[j][3])
        gate = [grad]
        if k == 0:
            gate = [grad, moved]
            moved = heads.scatter(gate)
    gate = [gate, moved]
    moved = heads.gather(gate)
    tokens_grad = call_input_gradient(after(dh1, gate), dqkvs, packs)
    heads.share(tokens_grad)
    query_grad, key_grad, value_grad, output_grad, sums = call_assemble(
        place_arg, heads.pieces(), width
    )
    return (
        layer_out,
        tokens_grad,
        query_grad.T,
        key_grad.T,
        value_grad.T,
        sums[8, :width],
        sums[8, 2 * width : 3 * width],
        output_grad,
        sums[5],
        sums[3],
        sums[4],
        inner_grad,
        sums[6, :hidden],
        down_grad,
        sums[2],
        sums[0],
        sums[1],
    )


def solution(mesh):
    whole_rows, columns, lines, split = P("dp", None), P(None, "tensor"), P("tensor", None), P("tensor")
    in_specs = (
        whole_rows, P("dp"), columns, columns, columns, split, split, lines, P(), P(), P(),
        columns, split, lines, P(), P(), P(), whole_rows,
    )
    out_specs = (
        whole_rows, whole_rows, columns, columns, columns, split, split, lines, P(), P(), P(),
        columns, split, lines, P(), P(), P(),
    )
    body = functools.partial(per_device, mesh.shape["tensor"], mesh.shape["dp"])
    return jax.shard_map(body, mesh=mesh, in_specs=in_specs, out_specs=out_specs, check_vma=False)
```

```python
import functools
import math

import jax
import jax.numpy as jnp
from jax import lax
from jax.experimental import pallas as pl
from jax.experimental.pallas import tpu as pltpu
from jax.sharding import PartitionSpec as P

HEAD_DIM = 64
SEQ_LEN = 512
EPS = 1e-06
MASKED = -1000000000.0
LANES = 8
LOW = jnp.bfloat16
WIDE = jnp.float32
VMEM_LIMIT = 26 * 1024 * 1024

NN = (((1,), (0,)), ((), ()))
NT = (((1,), (1,)), ((), ()))


def dot(left, right, dims):
    return lax.dot_general(left, right, dims, preferred_element_type=WIDE)


def params(limit=VMEM_LIMIT):
    return pltpu.CompilerParams(vmem_limit_bytes=limit)


def cost(count):
    return pl.CostEstimate(flops=7_500_000 * count, bytes_accessed=8192 * count, transcendentals=0)


def whole(shape):
    zeros = (0,) * len(shape)
    return pl.BlockSpec(shape, lambda i: zeros)


def rows(block, width):
    return pl.BlockSpec((block, width), lambda i: (i, 0))


def head_mask(width, head):
    lane = lax.broadcasted_iota(jnp.int32, (1, width), 1)
    return (lane >= head * HEAD_DIM) & (lane < (head + 1) * HEAD_DIM)


def same_document(seg_col, seg_row):
    return jnp.where(seg_col == seg_row, jnp.float32(3e38), jnp.float32(MASKED))


def attend_forward(remote, width, x_ref, scol_ref, srow_ref, *rest):
    if remote:
        place_ref, slices, rest = rest[0], rest[1 : 1 + LANES], rest[1 + LANES :]
        qkv_ref, c_ref, l_ref, w_ref, wide_ref = rest
        part = width // LANES
        bias = slices[0][4 * part : 4 * part + 1, : 3 * width]

        @pl.when(pl.program_id(0) == 0)
        def _():
            here = place_ref[0]
            for m in range(LANES):
                spot = here ^ m
                for t in range(4):
                    at = pl.multiple_of(t * width + spot * part, 8)
                    wide_ref[pl.ds(at, part), :] = slices[m][t * part : (t + 1) * part, :]
            w_ref[...] = wide_ref[...].astype(LOW)
    else:
        bias_ref, w_ref, qkv_ref, c_ref, l_ref = rest
        bias = bias_ref[...]
    heads = width // HEAD_DIM
    qkv = dot(x_ref[...], w_ref[: 3 * width, :], NT) + bias
    qkv = qkv.astype(LOW)
    qkv_ref[...] = qkv
    queries = qkv[:, :width] * LOW(HEAD_DIM**-0.5)
    keys = qkv[:, width : 2 * width]
    values_t = qkv[:, 2 * width :].T
    limit = same_document(scol_ref[...], srow_ref[0])
    parts = []
    for h in range(heads):
        key_h = jnp.where(head_mask(width, h), keys, LOW(0))
        scores = jnp.minimum(dot(key_h, queries, NT), limit)
        top = jnp.max(scores, axis=0, keepdims=True)
        weights = jnp.exp(scores - top)
        total = jnp.sum(weights, axis=0, keepdims=True)
        l_ref[0, h : h + 1, :] = top + jnp.log(total)
        value_h = values_t[h * HEAD_DIM : (h + 1) * HEAD_DIM, :]
        parts.append(dot(value_h, weights.astype(LOW), NN) / total)
    c_ref[...] = jnp.concatenate(parts, axis=0).T.astype(LOW)


def attend_backward(width, own, qkv_ref, c_ref, l_ref, scol_ref, srow_ref, da_ref, w_ref, dqkv_ref, *rest):
    heads = width // HEAD_DIM
    qkv = qkv_ref[...]
    queries = qkv[:, :width] * LOW(HEAD_DIM**-0.5)
    keys = qkv[:, width : 2 * width]
    values = qkv[:, 2 * width :]
    keys_t = keys.T
    dc = dot(da_ref[...], w_ref[...], NT).astype(LOW)
    prod_t = (dc.astype(WIDE) * c_ref[...].astype(WIDE)).T
    limit = same_document(scol_ref[...], srow_ref[0])
    dq_parts = []
    dk = jnp.zeros((SEQ_LEN, width), WIDE)
    dv = jnp.zeros((SEQ_LEN, width), WIDE)
    for h in range(heads):
        mask = head_mask(width, h)
        key_h = jnp.where(mask, keys, LOW(0))
        query_h = jnp.where(mask, queries, LOW(0))
        value_h = jnp.where(mask, values, LOW(0))
        dc_h = jnp.where(mask, dc, LOW(0))
        scores = jnp.minimum(dot(key_h, queries, NT), limit)
        probs = jnp.exp(scores - l_ref[0, h : h + 1, :])
        dprobs = dot(value_h, dc, NT)
        delta = jnp.sum(prod_t[h * HEAD_DIM : (h + 1) * HEAD_DIM, :], axis=0, keepdims=True)
        dscores = (probs * (dprobs - delta)).astype(LOW)
        dv = dv + dot(probs.astype(LOW), dc_h, NN)
        dk = dk + dot(dscores, query_h, NN)
        dq_parts.append(dot(keys_t[h * HEAD_DIM : (h + 1) * HEAD_DIM, :], dscores, NN))
    dq = jnp.concatenate(dq_parts, axis=0).T * (HEAD_DIM**-0.5)
    dqkv = jnp.concatenate([dq, dk, dv], axis=1).astype(LOW)
    dqkv_ref[...] = dqkv
    if own:
        sum_ref = rest[0]

        @pl.when(pl.program_id(0) == 0)
        def _():
            sum_ref[...] = jnp.zeros_like(sum_ref)

        sum_ref[0:1, : 3 * width] += column_sum(dqkv.astype(WIDE))


def call_attend_forward(width, tokens, scol, srow, bias, weight, place, slices):
    count, model = tokens.shape
    seqs = count // SEQ_LEN
    remote = slices is not None
    in_specs = [
        rows(SEQ_LEN, model),
        rows(SEQ_LEN, 1),
        pl.BlockSpec((1, 1, SEQ_LEN), lambda i: (i, 0, 0)),
    ]
    out_specs = [
        rows(SEQ_LEN, 3 * width),
        rows(SEQ_LEN, width),
        pl.BlockSpec((1, 8, SEQ_LEN), lambda i: (i, 0, 0)),
    ]
    out_shape = [
        jax.ShapeDtypeStruct((count, 3 * width), LOW),
        jax.ShapeDtypeStruct((count, width), LOW),
        jax.ShapeDtypeStruct((seqs, 8, SEQ_LEN), WIDE),
    ]
    scratch = []
    if remote:
        in_specs += [pl.BlockSpec(memory_space=pltpu.SMEM)]
        in_specs += [whole(slices[0].shape)] * LANES
        out_specs += [whole((4 * width, model))]
        out_shape += [jax.ShapeDtypeStruct((4 * width, model), LOW)]
        scratch = [pltpu.VMEM((4 * width, model), WIDE)]
        extra = (place, *slices)
    else:
        in_specs += [whole((1, 3 * width)), whole((4 * width, model))]
        extra = (bias, weight)
    return pl.pallas_call(
        functools.partial(attend_forward, remote, width),
        grid=(seqs,),
        in_specs=in_specs,
        out_specs=out_specs,
        out_shape=out_shape,
        scratch_shapes=scratch,
        compiler_params=params(),
        cost_estimate=cost(count),
    )(tokens, scol, srow, *extra)


def call_attend_backward(own, qkv, context, logs, scol, srow, da, weight):
    count, model = da.shape
    width = context.shape[1]
    seqs = count // SEQ_LEN
    in_specs = [
        rows(SEQ_LEN, 3 * width),
        rows(SEQ_LEN, width),
        pl.BlockSpec((1, 8, SEQ_LEN), lambda i: (i, 0, 0)),
        rows(SEQ_LEN, 1),
        pl.BlockSpec((1, 1, SEQ_LEN), lambda i: (i, 0, 0)),
        rows(SEQ_LEN, model),
        pl.BlockSpec((width, model), lambda i: (3, 0)),
    ]
    out_specs = [rows(SEQ_LEN, 3 * width)]
    out_shape = [jax.ShapeDtypeStruct((count, 3 * width), LOW)]
    if own:
        out_specs += [whole((8, model))]
        out_shape += [jax.ShapeDtypeStruct((8, model), WIDE)]
    return pl.pallas_call(
        functools.partial(attend_backward, width, own),
        grid=(seqs,),
        in_specs=in_specs,
        out_specs=out_specs,
        out_shape=out_shape,
        compiler_params=params(),
        cost_estimate=cost(count),
    )(qkv, context, logs, scol, srow, da, weight)


def input_gradient(groups, dh1_ref, *rest):
    dqkvs, weights, out_ref = rest[:groups], rest[groups : 2 * groups], rest[2 * groups]
    total = dh1_ref[...]
    for dqkv, weight in zip(dqkvs, weights):
        total = total + dot(dqkv[...], weight[: dqkv.shape[1], :], NN)
    out_ref[...] = total


def call_input_gradient(dh1, dqkvs, weights, block=512):
    count, model = dh1.shape
    groups = len(dqkvs)
    wide = dqkvs[0].shape[1]
    once = pl.BlockSpec((wide, model), lambda i: (0, 0), pipeline_mode=pl.Buffered(1))
    return pl.pallas_call(
        functools.partial(input_gradient, groups),
        grid=(count // block,),
        in_specs=[rows(block, model)] + [rows(block, wide)] * groups + [once] * groups,
        out_specs=rows(block, model),
        input_output_aliases={0: 0},
        out_shape=jax.ShapeDtypeStruct((count, model), WIDE),
        compiler_params=params(),
        cost_estimate=cost(count),
    )(dh1, *dqkvs, *weights)


def gelu_pair(u):
    tail = jnp.exp(u * u * -0.5)
    t = 1.0 / (1.0 + jnp.abs(u) * (0.3275911 * math.sqrt(0.5)))
    poly = 0.5 * 1.061405429
    for c in (-1.453152027, 1.421413741, -0.284496736, 0.254829592):
        poly = poly * t + 0.5 * c
    half = poly * t * tail
    phi = jnp.where(u < 0.0, half, 1.0 - half)
    return u * phi, phi + u * tail * (1.0 / math.sqrt(2.0 * math.pi))


def stats(values):
    mean = jnp.mean(values, axis=1, keepdims=True)
    center = values - mean
    scale = lax.rsqrt(jnp.mean(center * center, axis=1, keepdims=True) + EPS)
    return center * scale, scale


def feed_forward(remote, x_ref, *rest):
    if remote:
        acc_ref, rest = rest[0], rest[1:]
        place_ref, slices, rest = rest[0], rest[1 : 1 + LANES], rest[1 + LANES :]
        slope_ref, out_ref, wi_ref, wd_ref = rest
        part = wi_ref.shape[0] // LANES
        bias = slices[0][2 * part : 2 * part + 1, : wi_ref.shape[0]]

        @pl.when(pl.program_id(0) == 0)
        def _():
            here = place_ref[0]
            for m in range(LANES):
                at = pl.multiple_of((here ^ m) * part, part)
                wi_ref[pl.ds(at, part), :] = slices[m][:part, :].astype(LOW)
                wd_ref[pl.ds(at, part), :] = slices[m][part : 2 * part, :].astype(LOW)

        normed_low = x_ref[...]
    else:
        bias_ref, wi_ref, wd_ref, slope_ref, out_ref, act_ref = rest
        bias = bias_ref[...]
        normed_low = x_ref[...]
    hidden = wi_ref.shape[0]
    chunk = 768
    total = None
    for c in range(0, hidden, chunk):
        cols = slice(c, c + chunk)
        u = dot(normed_low, wi_ref[cols, :], NT) + bias[:, cols]
        act, slope = gelu_pair(u)
        act = act.astype(LOW)
        slope_ref[:, cols] = slope.astype(LOW)
        if not remote:
            act_ref[:, cols] = act
        add = dot(act, wd_ref[cols, :], NN)
        total = add if total is None else total + add
    out_ref[...] = total if not remote else acc_ref[...] + total


def call_feed_forward(hidden, x, remote, extra, block=512):
    count, model = x.shape
    in_specs = [rows(block, model)]
    out_specs = [rows(block, hidden), rows(block, model)]
    out_shape = [
        jax.ShapeDtypeStruct((count, hidden), LOW),
        jax.ShapeDtypeStruct((count, model), WIDE),
    ]
    if remote:
        in_specs += [rows(block, model), pl.BlockSpec(memory_space=pltpu.SMEM)]
        in_specs += [whole(extra[2].shape)] * LANES
        out_specs += [whole((hidden, model))] * 2
        out_shape += [jax.ShapeDtypeStruct((hidden, model), LOW)] * 2
    else:
        in_specs += [whole((1, hidden))] + [whole((hidden, model))] * 2
        out_specs += [rows(block, hidden)]
        out_shape += [jax.ShapeDtypeStruct((count, hidden), LOW)]
    return pl.pallas_call(
        functools.partial(feed_forward, remote),
        grid=(count // block,),
        in_specs=in_specs,
        out_specs=out_specs,
        out_shape=out_shape,
        input_output_aliases={1: 1} if remote else {},
        compiler_params=params((61 if remote else 26) * 1024 * 1024),
        cost_estimate=cost(count),
    )(x, *extra)


GAIN_ONE, SHIFT_ONE, DOWN_BIAS, GAIN_TWO, SHIFT_TWO, OUT_BIAS = range(6)


def vector(vec_ref, at):
    return vec_ref[at : at + 1, :]


def first_norm(groups, x_ref, vec_ref, *rest):
    contexts, outs, (h1_ref, n1_ref) = rest[:groups], rest[groups : 2 * groups], rest[2 * groups :]
    h1 = x_ref[...].astype(WIDE) + vector(vec_ref, OUT_BIAS)
    for context, weight in zip(contexts, outs):
        h1 = h1 + dot(context[...], weight[...], NN)
    h1_ref[...] = h1
    hat, _ = stats(h1)
    n1_ref[...] = (hat * vector(vec_ref, GAIN_ONE) + vector(vec_ref, SHIFT_ONE)).astype(LOW)


def call_first_norm(tokens, vec, contexts, packs, block=512):
    count, model = tokens.shape
    groups = len(contexts)
    width = contexts[0].shape[1]
    return pl.pallas_call(
        functools.partial(first_norm, groups),
        grid=(count // block,),
        in_specs=[rows(block, model), whole(vec.shape)]
        + [rows(block, width)] * groups
        + [pl.BlockSpec((width, model), lambda i: (3, 0))] * groups,
        out_specs=[rows(block, model)] * 2,
        out_shape=[jax.ShapeDtypeStruct((count, model), WIDE), jax.ShapeDtypeStruct((count, model), LOW)],
        compiler_params=params(),
        cost_estimate=cost(count),
    )(tokens, vec, *contexts, *packs)


def norm_back(grad, hat, scale, gain):
    d = grad * gain
    first = jnp.mean(d, axis=1, keepdims=True)
    second = jnp.mean(d * hat, axis=1, keepdims=True)
    return scale * (d - first - hat * second)


def column_sum(values):
    return jnp.sum(values, axis=0, keepdims=True)


def back_through(dm, slope, wi_ref, wd_ref, dn1, keep=None):
    chunk = 768
    for c in range(0, wi_ref.shape[0], chunk):
        cols = slice(c, c + chunk)
        dact = dot(dm, wd_ref[cols, :], NT)
        du = (dact * slope[:, cols].astype(WIDE)).astype(LOW)
        if keep is not None:
            keep(cols, du)
        dn1 = dn1 + dot(du, wi_ref[cols, :], NN)
    return dn1


def middle_own(h1_ref, m_ref, cot_ref, vec_ref, slope_ref, wi_ref, wd_ref, act_ref, n1_ref, *outs):
    layer_ref, dm_ref, dn1_ref, sums_ref, down_ref, inner_ref = outs

    @pl.when(pl.program_id(0) == 0)
    def _():
        sums_ref[...] = jnp.zeros_like(sums_ref)
        down_ref[...] = jnp.zeros_like(down_ref)
        inner_ref[...] = jnp.zeros_like(inner_ref)

    hat1, _ = stats(h1_ref[...])
    normed = hat1 * vector(vec_ref, GAIN_ONE) + vector(vec_ref, SHIFT_ONE)
    hat2, scale2 = stats(normed + m_ref[...] + vector(vec_ref, DOWN_BIAS))
    layer_ref[...] = (hat2 * vector(vec_ref, GAIN_TWO) + vector(vec_ref, SHIFT_TWO)).astype(LOW)
    up = cot_ref[...].astype(WIDE)
    sums_ref[0:1, :] += column_sum(up * hat2)
    sums_ref[1:2, :] += column_sum(up)
    dh2 = norm_back(up, hat2, scale2, vector(vec_ref, GAIN_TWO))
    sums_ref[2:3, :] += column_sum(dh2)
    dm = dh2.astype(LOW)
    dm_ref[...] = dm
    down_ref[...] += inner_first(act_ref[...], dm)

    def keep(cols, du):
        inner_ref[:, cols] += inner_first(n1_ref[...], du)
        sums_ref[6:7, cols] += column_sum(du.astype(WIDE))

    dn1_ref[...] = back_through(dm, slope_ref, wi_ref, wd_ref, dh2, keep)


def middle_rest(groups, h1_ref, dn1_ref, dm_ref, vec_ref, old_ref, *rest):
    slopes, wis, wds = rest[:groups], rest[groups : 2 * groups], rest[2 * groups : 3 * groups]
    dh1_ref, da_ref, sums_ref = rest[3 * groups :]

    @pl.when(pl.program_id(0) == 0)
    def _():
        sums_ref[...] = old_ref[...]

    hat1, scale1 = stats(h1_ref[...])
    dm = dm_ref[...]
    dn1 = dn1_ref[...]
    for slope_ref, wi_ref, wd_ref in zip(slopes, wis, wds):
        dn1 = back_through(dm, slope_ref, wi_ref, wd_ref, dn1)
    sums_ref[3:4, :] += column_sum(dn1 * hat1)
    sums_ref[4:5, :] += column_sum(dn1)
    dh1 = norm_back(dn1, hat1, scale1, vector(vec_ref, GAIN_ONE))
    sums_ref[5:6, :] += column_sum(dh1)
    dh1_ref[...] = dh1
    da_ref[...] = dh1.astype(LOW)


def call_middle_own(h1, mixed, cot, vec, slope, wi, wd, act, n1, block=512):
    count, model = h1.shape
    hidden = wi.shape[0]
    once = pl.BlockSpec((hidden, model), lambda i: (0, 0), pipeline_mode=pl.Buffered(1))
    return pl.pallas_call(
        middle_own,
        grid=(count // block,),
        in_specs=[rows(block, model)] * 3 + [whole(vec.shape), rows(block, hidden)] + [once] * 2
        + [rows(block, hidden), rows(block, model)],
        out_specs=[rows(block, model)] * 3 + [whole((8, model)), whole((hidden, model)), whole((model, hidden))],
        out_shape=[
            jax.ShapeDtypeStruct((count, model), LOW),
            jax.ShapeDtypeStruct((count, model), LOW),
            jax.ShapeDtypeStruct((count, model), WIDE),
            jax.ShapeDtypeStruct((8, model), WIDE),
            jax.ShapeDtypeStruct((hidden, model), WIDE),
            jax.ShapeDtypeStruct((model, hidden), WIDE),
        ],
        input_output_aliases={1: 2},
        compiler_params=params(61 * 1024 * 1024),
        cost_estimate=cost(count),
    )(h1, mixed, cot, vec, slope, wi, wd, act, n1)


def call_middle_rest(h1, dn1, dm, vec, sums, slopes, wis, wds, block=512):
    count, model = h1.shape
    groups = len(slopes)
    hidden = wis[0].shape[0]
    once = pl.BlockSpec((hidden, model), lambda i: (0, 0), pipeline_mode=pl.Buffered(1))
    return pl.pallas_call(
        functools.partial(middle_rest, groups),
        grid=(count // block,),
        in_specs=[rows(block, model)] * 3
        + [whole(vec.shape), whole((8, model))]
        + [rows(block, hidden)] * groups
        + [once] * (2 * groups),
        out_specs=[rows(block, model), rows(block, model), whole((8, model))],
        out_shape=[
            jax.ShapeDtypeStruct((count, model), WIDE),
            jax.ShapeDtypeStruct((count, model), LOW),
            jax.ShapeDtypeStruct((8, model), WIDE),
        ],
        input_output_aliases={1: 0},
        compiler_params=params(61 * 1024 * 1024),
        cost_estimate=cost(count),
    )(h1, dn1, dm, vec, sums, *slopes, *wis, *wds)


def inner_first(left, right):
    return lax.dot_general(left, right, (((0,), (0,)), ((), ())), preferred_element_type=WIDE)


def assemble(place_ref, *rest):
    pieces, outs, out_ref = rest[:LANES], rest[LANES:-1], rest[-1]
    part = pieces[0].shape[0]
    core, chip = place_ref[0] % 2, place_ref[0] // 2
    for k, piece in enumerate(pieces):
        half = core if k < 4 else 1 - core
        at = pl.multiple_of((half * 4 + (chip ^ (k % 4))) * part, 8)
        out_ref[pl.ds(at, part), :] = piece[...]
    width = outs[3].shape[0]
    for k in range(4):
        outs[k][...] = out_ref[k * width : (k + 1) * width, :]
    outs[4][...] = out_ref[4 * width : 4 * width + 16, :]


def call_assemble(place, pieces, width):
    part, model = pieces[0].shape
    shapes = [(width, model)] * 4 + [(16, model)]
    return pl.pallas_call(
        assemble,
        grid=(1,),
        in_specs=[pl.BlockSpec(memory_space=pltpu.SMEM)] + [whole((part, model))] * LANES,
        out_specs=[whole(shape) for shape in shapes],
        out_shape=[jax.ShapeDtypeStruct(shape, WIDE) for shape in shapes],
        scratch_shapes=[pltpu.VMEM((part * LANES, model), WIDE)],
        compiler_params=params(),
    )(place, *pieces)


def after(values, *done):
    return lax.optimization_barrier((values, done))[0]


def swap(value, mask, size):
    return lax.ppermute(value, "dp", [(i, i ^ mask) for i in range(size)])


def from_tensor(value, shift, groups):
    return lax.ppermute(value, "tensor", [((i + shift) % groups, i) for i in range(groups)])


class Spread:
    def __init__(self, piece, shift, groups, size):
        self.piece, self.shift, self.groups, self.size = piece, shift, groups, size
        self.got = {}

    def along(self, *done):
        self.got[0] = from_tensor(after(self.piece, *done), self.shift, self.groups)
        return self.got[0]

    def hop(self, m, mask, *done):
        self.got[m ^ mask] = swap(after(self.got[m], *done), mask, self.size)
        return self.got[m ^ mask]

    def slices(self):
        return [self.got[m] for m in range(LANES)]


class Total:
    def __init__(self, value, size):
        self.value, self.size = value, size
        self.me = lax.axis_index("dp")
        self.half = value.shape[0] // 2
        self.part = self.half // 4

    def cut(self, value, at, count):
        return lax.dynamic_slice(value, (at, 0), (count, value.shape[1]))

    def pair(self, *done):
        value = after(self.value, *done)
        core = self.me % 2
        self.kept = self.cut(value, core * self.half, self.half)
        self.come = swap(self.cut(value, (1 - core) * self.half, self.half), 1, self.size)
        return self.come

    def scatter(self, *done):
        half = self.kept + after(self.come, *done)
        spot = (self.me // 2) % 4
        parts = [self.cut(half, (spot ^ m) * self.part, self.part) for m in range(4)]
        self.got = [parts[0]] + [swap(parts[m], 2 * m, self.size) for m in (1, 2, 3)]
        return self.got

    def gather(self, *done):
        a, b, c, d = after(self.got, *done)
        total = (a + b) + (c + d)
        mask = LANES
        while mask < self.size:
            total = total + swap(total, mask, self.size)
            mask *= 2
        self.got = [total] + [swap(total, 2 * m, self.size) for m in (1, 2, 3)]
        return self.got

    def share(self, *done):
        self.got = list(after(self.got, *done))
        self.other = [swap(part, 1, self.size) for part in self.got]
        return self.other

    def pieces(self):
        return [*self.got, *self.other]


def per_device(
    groups,
    size,
    tokens,
    segments,
    query_weight,
    key_weight,
    value_weight,
    query_bias,
    value_bias,
    output_weight,
    output_bias,
    gain_one,
    shift_one,
    inner_weight,
    inner_bias,
    down_weight,
    down_bias,
    gain_two,
    shift_two,
    cotangent,
):
    count, model = tokens.shape
    width = query_weight.shape[1]
    hidden = inner_weight.shape[1]
    place = (lax.axis_index("dp") % LANES).astype(jnp.int32)
    place_arg = place.reshape(1)
    others = range(1, groups)
    row = lambda v: v.reshape(1, -1)

    qkvo = jnp.concatenate([query_weight.T, key_weight.T, value_weight.T, output_weight], axis=0)
    inner_t = inner_weight.T
    narrow, deep = width // LANES, hidden // LANES

    def bias_rows(values):
        return jnp.pad(row(values), ((0, 7), (0, model - values.shape[0])))

    head_bias = jnp.concatenate([query_bias, jnp.zeros_like(query_bias), value_bias])
    head_piece = jnp.concatenate(
        [
            lax.dynamic_slice(
                qkvo.reshape(4, width, model), (0, place * narrow, 0), (4, narrow, model)
            ).reshape(4 * narrow, model).astype(WIDE),
            bias_rows(head_bias),
        ],
        axis=0,
    )
    deep_piece = jnp.concatenate(
        [
            lax.dynamic_slice(inner_t, (place * deep, 0), (deep, model)).astype(WIDE),
            lax.dynamic_slice(down_weight, (place * deep, 0), (deep, model)).astype(WIDE),
            bias_rows(inner_bias),
        ],
        axis=0,
    )
    vec = jnp.stack([gain_one, shift_one, down_bias, gain_two, shift_two, output_bias, output_bias, output_bias])
    scol = segments.reshape(count, 1)
    srow = segments.reshape(count // SEQ_LEN, 1, SEQ_LEN)

    order = [j for j in others if j % 2] + [j for j in others if j % 2 == 0]
    head_of = [Spread(head_piece, j, groups, size) for j in order]
    deep_of = [Spread(deep_piece, j, groups, size) for j in order]
    saved = {}

    def forward(k, *done):
        if k < 0:
            out = call_attend_forward(
                width, after(tokens, *done), scol, srow, row(head_bias), qkvo, None, None
            )
            saved[0] = (*out, qkvo)
        else:
            slices = after(head_of[k].slices(), *done)
            out = call_attend_forward(width, tokens, scol, srow, None, None, place_arg, slices)
            saved[order[k]] = out
        return out[2]

    a, b, c = head_of
    d, e, f = deep_of
    gate = [a.along()]
    late = c.along(gate)
    gate = [
        a.hop(0, 2, gate), a.hop(0, 4, gate), a.hop(0, 6, gate), b.along(gate), forward(-1, gate, deep_piece)
    ]
    gate = [a.hop(m, 1, gate) for m in (0, 2, 4, 6)] + [late]
    late = d.along(gate)
    gate = [forward(0, gate), b.hop(0, 2, gate), b.hop(0, 4, gate), b.hop(0, 6, gate), b.hop(0, 1, gate)]
    later = e.along(gate)
    gate = [b.hop(m, 1, gate) for m in (2, 4, 6)] + [late]
    gate = [forward(1, gate), c.hop(0, 2, gate), c.hop(0, 4, gate), c.hop(0, 6, gate), c.hop(0, 1, gate), later]
    begun = [d.hop(0, 2, gate), d.hop(0, 4, gate)]
    gate = [c.hop(m, 1, gate) for m in (2, 4, 6)]
    late = [f.along(gate), e.hop(0, 2, gate)]
    gate = [forward(2, gate), begun, d.hop(0, 1, gate)]
    contexts, packs = [saved[j][1] for j in range(groups)], [saved[j][3] for j in range(groups)]
    h1, n1 = call_first_norm(after(tokens, gate), vec, contexts, packs)
    slopes, wis, wds = [], [inner_t], [down_weight]

    def deep_forward(k, mixed, *done):
        slices = after(deep_of[k].slices(), *done)
        slope, mixed, wi, wd = call_feed_forward(hidden, n1, True, (mixed, place_arg, *slices))
        slopes.append(slope)
        wis.append(wi)
        wds.append(wd)
        return slope, mixed

    begun = [d.hop(2, 4, gate), d.hop(2, 1, gate), e.hop(0, 4, gate)]
    gate = [n1, late]
    begun += [f.hop(0, 2, gate), e.hop(0, 1, gate)]
    slope, mixed, act = call_feed_forward(
        hidden, after(n1, gate), False, (row(inner_bias), inner_t, down_weight)
    )
    slopes.append(slope)
    gate = [slope, begun]
    begun = [f.hop(0, 4, gate), e.hop(4, 2, gate), e.hop(2, 1, gate)]
    gate = [d.hop(4, 1, gate), d.hop(6, 1, gate)]
    slope, mixed = deep_forward(0, mixed, gate)
    gate = [slope, begun]
    begun = [f.hop(2, 4, gate), f.hop(0, 1, gate), f.hop(2, 1, gate)]
    gate = [e.hop(4, 1, gate), e.hop(6, 1, gate)]
    slope, mixed = deep_forward(1, mixed, gate)
    gate = [slope, begun]
    gate = [f.hop(4, 1, gate), f.hop(6, 1, gate)]
    slope, mixed = deep_forward(2, mixed, gate)

    layer_out, dm, dn1, sums, *own = call_middle_own(
        h1, mixed, cotangent, vec, slopes[0], wis[0], wds[0], act, n1
    )

    own = after(tuple(own), dm)
    down_grad, inner_grad = lax.psum(own, "dp")
    dh1, da, sums = call_middle_rest(h1, after(dn1, own), dm, vec, sums, slopes[1:], wis[1:], wds[1:])

    def backward(j, *done):
        qkv, context, logs, pack = saved[j]
        return call_attend_backward(j == 0, qkv, context, logs, scol, srow, after(da, *done), pack)

    dqkv0, qkv_sums = backward(0)
    parts = [inner_first(dqkv0, tokens), inner_first(saved[0][1], da), sums, qkv_sums]
    used = sum(part.shape[0] for part in parts)
    parts.append(jnp.zeros((-used % (8 * LANES), model), WIDE))
    heads = Total(jnp.concatenate(parts, axis=0), size)
    gate = [heads.value]
    dqkvs, packs = [dqkv0], [qkvo]
    moved = heads.pair(gate)
    for k, j in enumerate(order):
        (grad,) = backward(j, gate)
        dqkvs.append(grad)
        packs.append(saved[j][3])
        gate = [grad]
        if k == 0:
            gate = [grad, moved]
            moved = heads.scatter(gate)
    gate = [gate, moved]
    moved = heads.gather(gate)
    tokens_grad = call_input_gradient(after(dh1, gate), dqkvs, packs)
    heads.share(tokens_grad)
    query_grad, key_grad, value_grad, output_grad, sums = call_assemble(
        place_arg, heads.pieces(), width
    )
    return (
        layer_out,
        tokens_grad,
        query_grad.T,
        key_grad.T,
        value_grad.T,
        sums[8, :width],
        sums[8, 2 * width : 3 * width],
        output_grad,
        sums[5],
        sums[3],
        sums[4],
        inner_grad,
        sums[6, :hidden],
        down_grad,
        sums[2],
        sums[0],
        sums[1],
    )


def solution(mesh):
    whole_rows, columns, lines, split = P("dp", None), P(None, "tensor"), P("tensor", None), P("tensor")
    in_specs = (
        whole_rows, P("dp"), columns, columns, columns, split, split, lines, P(), P(), P(),
        columns, split, lines, P(), P(), P(), whole_rows,
    )
    out_specs = (
        whole_rows, whole_rows, columns, columns, columns, split, split, lines, P(), P(), P(),
        columns, split, lines, P(), P(), P(),
    )
    body = functools.partial(per_device, mesh.shape["tensor"], mesh.shape["dp"])
    return jax.shard_map(body, mesh=mesh, in_specs=in_specs, out_specs=out_specs, check_vma=False)
```

```python
import functools
import math

import jax
import jax.numpy as jnp
from jax import lax
from jax.experimental import pallas as pl
from jax.experimental.pallas import tpu as pltpu
from jax.sharding import PartitionSpec as P

HEAD_DIM = 64
SEQ_LEN = 512
EPS = 1e-06
MASKED = -1000000000.0
LANES = 8
LOW = jnp.bfloat16
WIDE = jnp.float32
VMEM_LIMIT = 26 * 1024 * 1024

NN = (((1,), (0,)), ((), ()))
NT = (((1,), (1,)), ((), ()))


def dot(left, right, dims):
    return lax.dot_general(left, right, dims, preferred_element_type=WIDE)


def params(limit=VMEM_LIMIT):
    return pltpu.CompilerParams(vmem_limit_bytes=limit)


def cost(count):
    return pl.CostEstimate(flops=7_500_000 * count, bytes_accessed=8192 * count, transcendentals=0)


def whole(shape):
    zeros = (0,) * len(shape)
    return pl.BlockSpec(shape, lambda i: zeros)


def rows(block, width):
    return pl.BlockSpec((block, width), lambda i: (i, 0))


def head_mask(width, head):
    lane = lax.broadcasted_iota(jnp.int32, (1, width), 1)
    return (lane >= head * HEAD_DIM) & (lane < (head + 1) * HEAD_DIM)


def same_document(seg_col, seg_row):
    return jnp.where(seg_col == seg_row, jnp.float32(3e38), jnp.float32(MASKED))


def attend_forward(remote, width, x_ref, scol_ref, srow_ref, *rest):
    if remote:
        place_ref, slices, rest = rest[0], rest[1 : 1 + LANES], rest[1 + LANES :]
        qkv_ref, c_ref, l_ref, w_ref, wide_ref = rest
        part = width // LANES
        bias = slices[0][4 * part : 4 * part + 1, : 3 * width]

        @pl.when(pl.program_id(0) == 0)
        def _():
            here = place_ref[0]
            for m in range(LANES):
                spot = here ^ m
                for t in range(4):
                    at = pl.multiple_of(t * width + spot * part, 8)
                    wide_ref[pl.ds(at, part), :] = slices[m][t * part : (t + 1) * part, :]
            w_ref[...] = wide_ref[...].astype(LOW)
    else:
        bias_ref, w_ref, qkv_ref, c_ref, l_ref = rest
        bias = bias_ref[...]
    heads = width // HEAD_DIM
    qkv = dot(x_ref[...], w_ref[: 3 * width, :], NT) + bias
    qkv = qkv.astype(LOW)
    qkv_ref[...] = qkv
    queries = qkv[:, :width] * LOW(HEAD_DIM**-0.5)
    keys = qkv[:, width : 2 * width]
    values_t = qkv[:, 2 * width :].T
    limit = same_document(scol_ref[...], srow_ref[0])
    parts = []
    for h in range(heads):
        key_h = jnp.where(head_mask(width, h), keys, LOW(0))
        scores = jnp.minimum(dot(key_h, queries, NT), limit)
        top = jnp.max(scores, axis=0, keepdims=True)
        weights = jnp.exp(scores - top)
        total = jnp.sum(weights, axis=0, keepdims=True)
        l_ref[0, h : h + 1, :] = top + jnp.log(total)
        value_h = values_t[h * HEAD_DIM : (h + 1) * HEAD_DIM, :]
        parts.append(dot(value_h, weights.astype(LOW), NN) / total)
    c_ref[...] = jnp.concatenate(parts, axis=0).T.astype(LOW)


def attend_backward(width, own, qkv_ref, c_ref, l_ref, scol_ref, srow_ref, da_ref, w_ref, dqkv_ref, *rest):
    heads = width // HEAD_DIM
    qkv = qkv_ref[...]
    queries = qkv[:, :width] * LOW(HEAD_DIM**-0.5)
    keys = qkv[:, width : 2 * width]
    values = qkv[:, 2 * width :]
    keys_t = keys.T
    dc = dot(da_ref[...], w_ref[...], NT).astype(LOW)
    prod_t = (dc.astype(WIDE) * c_ref[...].astype(WIDE)).T
    limit = same_document(scol_ref[...], srow_ref[0])
    dq_parts = []
    dk = jnp.zeros((SEQ_LEN, width), WIDE)
    dv = jnp.zeros((SEQ_LEN, width), WIDE)
    for h in range(heads):
        mask = head_mask(width, h)
        key_h = jnp.where(mask, keys, LOW(0))
        query_h = jnp.where(mask, queries, LOW(0))
        value_h = jnp.where(mask, values, LOW(0))
        dc_h = jnp.where(mask, dc, LOW(0))
        scores = jnp.minimum(dot(key_h, queries, NT), limit)
        probs = jnp.exp(scores - l_ref[0, h : h + 1, :])
        dprobs = dot(value_h, dc, NT)
        delta = jnp.sum(prod_t[h * HEAD_DIM : (h + 1) * HEAD_DIM, :], axis=0, keepdims=True)
        dscores = (probs * (dprobs - delta)).astype(LOW)
        dv = dv + dot(probs.astype(LOW), dc_h, NN)
        dk = dk + dot(dscores, query_h, NN)
        dq_parts.append(dot(keys_t[h * HEAD_DIM : (h + 1) * HEAD_DIM, :], dscores, NN))
    dq = jnp.concatenate(dq_parts, axis=0).T * (HEAD_DIM**-0.5)
    dqkv = jnp.concatenate([dq, dk, dv], axis=1).astype(LOW)
    dqkv_ref[...] = dqkv
    if own:
        sum_ref = rest[0]

        @pl.when(pl.program_id(0) == 0)
        def _():
            sum_ref[...] = jnp.zeros_like(sum_ref)

        sum_ref[0:1, : 3 * width] += column_sum(dqkv.astype(WIDE))


def call_attend_forward(width, tokens, scol, srow, bias, weight, place, slices):
    count, model = tokens.shape
    seqs = count // SEQ_LEN
    remote = slices is not None
    in_specs = [
        rows(SEQ_LEN, model),
        rows(SEQ_LEN, 1),
        pl.BlockSpec((1, 1, SEQ_LEN), lambda i: (i, 0, 0)),
    ]
    out_specs = [
        rows(SEQ_LEN, 3 * width),
        rows(SEQ_LEN, width),
        pl.BlockSpec((1, 8, SEQ_LEN), lambda i: (i, 0, 0)),
    ]
    out_shape = [
        jax.ShapeDtypeStruct((count, 3 * width), LOW),
        jax.ShapeDtypeStruct((count, width), LOW),
        jax.ShapeDtypeStruct((seqs, 8, SEQ_LEN), WIDE),
    ]
    scratch = []
    if remote:
        in_specs += [pl.BlockSpec(memory_space=pltpu.SMEM)]
        in_specs += [whole(slices[0].shape)] * LANES
        out_specs += [whole((4 * width, model))]
        out_shape += [jax.ShapeDtypeStruct((4 * width, model), LOW)]
        scratch = [pltpu.VMEM((4 * width, model), WIDE)]
        extra = (place, *slices)
    else:
        in_specs += [whole((1, 3 * width)), whole((4 * width, model))]
        extra = (bias, weight)
    return pl.pallas_call(
        functools.partial(attend_forward, remote, width),
        grid=(seqs,),
        in_specs=in_specs,
        out_specs=out_specs,
        out_shape=out_shape,
        scratch_shapes=scratch,
        compiler_params=params(),
        cost_estimate=cost(count),
    )(tokens, scol, srow, *extra)


def call_attend_backward(own, qkv, context, logs, scol, srow, da, weight):
    count, model = da.shape
    width = context.shape[1]
    seqs = count // SEQ_LEN
    in_specs = [
        rows(SEQ_LEN, 3 * width),
        rows(SEQ_LEN, width),
        pl.BlockSpec((1, 8, SEQ_LEN), lambda i: (i, 0, 0)),
        rows(SEQ_LEN, 1),
        pl.BlockSpec((1, 1, SEQ_LEN), lambda i: (i, 0, 0)),
        rows(SEQ_LEN, model),
        pl.BlockSpec((width, model), lambda i: (3, 0)),
    ]
    out_specs = [rows(SEQ_LEN, 3 * width)]
    out_shape = [jax.ShapeDtypeStruct((count, 3 * width), LOW)]
    if own:
        out_specs += [whole((8, model))]
        out_shape += [jax.ShapeDtypeStruct((8, model), WIDE)]
    return pl.pallas_call(
        functools.partial(attend_backward, width, own),
        grid=(seqs,),
        in_specs=in_specs,
        out_specs=out_specs,
        out_shape=out_shape,
        compiler_params=params((61 if own else 26) * 1024 * 1024),
        cost_estimate=cost(count),
    )(qkv, context, logs, scol, srow, da, weight)


def input_gradient(groups, dh1_ref, *rest):
    dqkvs, weights, out_ref = rest[:groups], rest[groups : 2 * groups], rest[2 * groups]
    total = dh1_ref[...]
    for dqkv, weight in zip(dqkvs, weights):
        total = total + dot(dqkv[...], weight[: dqkv.shape[1], :], NN)
    out_ref[...] = total


def call_input_gradient(dh1, dqkvs, weights, block=512):
    count, model = dh1.shape
    groups = len(dqkvs)
    wide = dqkvs[0].shape[1]
    once = pl.BlockSpec((wide, model), lambda i: (0, 0), pipeline_mode=pl.Buffered(1))
    return pl.pallas_call(
        functools.partial(input_gradient, groups),
        grid=(count // block,),
        in_specs=[rows(block, model)] + [rows(block, wide)] * groups + [once] * groups,
        out_specs=rows(block, model),
        input_output_aliases={0: 0},
        out_shape=jax.ShapeDtypeStruct((count, model), WIDE),
        compiler_params=params(),
        cost_estimate=cost(count),
    )(dh1, *dqkvs, *weights)


def gelu_pair(u):
    tail = jnp.exp(u * u * -0.5)
    t = 1.0 / (1.0 + jnp.abs(u) * (0.3275911 * math.sqrt(0.5)))
    poly = 0.5 * 1.061405429
    for c in (-1.453152027, 1.421413741, -0.284496736, 0.254829592):
        poly = poly * t + 0.5 * c
    half = poly * t * tail
    phi = jnp.where(u < 0.0, half, 1.0 - half)
    return u * phi, phi + u * tail * (1.0 / math.sqrt(2.0 * math.pi))


def stats(values):
    mean = jnp.mean(values, axis=1, keepdims=True)
    center = values - mean
    scale = lax.rsqrt(jnp.mean(center * center, axis=1, keepdims=True) + EPS)
    return center * scale, scale


def feed_forward(remote, x_ref, *rest):
    if remote:
        acc_ref, rest = rest[0], rest[1:]
        place_ref, slices, rest = rest[0], rest[1 : 1 + LANES], rest[1 + LANES :]
        slope_ref, out_ref, wi_ref, wd_ref = rest
        part = wi_ref.shape[0] // LANES
        bias = slices[0][2 * part : 2 * part + 1, : wi_ref.shape[0]]

        @pl.when(pl.program_id(0) == 0)
        def _():
            here = place_ref[0]
            for m in range(LANES):
                at = pl.multiple_of((here ^ m) * part, part)
                wi_ref[pl.ds(at, part), :] = slices[m][:part, :].astype(LOW)
                wd_ref[pl.ds(at, part), :] = slices[m][part : 2 * part, :].astype(LOW)

        normed_low = x_ref[...]
    else:
        bias_ref, wi_ref, wd_ref, slope_ref, out_ref, act_ref = rest
        bias = bias_ref[...]
        normed_low = x_ref[...]
    hidden = wi_ref.shape[0]
    chunk = 768
    total = None
    for c in range(0, hidden, chunk):
        cols = slice(c, c + chunk)
        u = dot(normed_low, wi_ref[cols, :], NT) + bias[:, cols]
        act, slope = gelu_pair(u)
        act = act.astype(LOW)
        slope_ref[:, cols] = slope.astype(LOW)
        if not remote:
            act_ref[:, cols] = act
        add = dot(act, wd_ref[cols, :], NN)
        total = add if total is None else total + add
    out_ref[...] = total if not remote else acc_ref[...] + total


def call_feed_forward(hidden, x, remote, extra, block=512):
    count, model = x.shape
    in_specs = [rows(block, model)]
    out_specs = [rows(block, hidden), rows(block, model)]
    out_shape = [
        jax.ShapeDtypeStruct((count, hidden), LOW),
        jax.ShapeDtypeStruct((count, model), WIDE),
    ]
    if remote:
        in_specs += [rows(block, model), pl.BlockSpec(memory_space=pltpu.SMEM)]
        in_specs += [whole(extra[2].shape)] * LANES
        out_specs += [whole((hidden, model))] * 2
        out_shape += [jax.ShapeDtypeStruct((hidden, model), LOW)] * 2
    else:
        in_specs += [whole((1, hidden))] + [whole((hidden, model))] * 2
        out_specs += [rows(block, hidden)]
        out_shape += [jax.ShapeDtypeStruct((count, hidden), LOW)]
    return pl.pallas_call(
        functools.partial(feed_forward, remote),
        grid=(count // block,),
        in_specs=in_specs,
        out_specs=out_specs,
        out_shape=out_shape,
        input_output_aliases={1: 1} if remote else {},
        compiler_params=params((61 if remote else 26) * 1024 * 1024),
        cost_estimate=cost(count),
    )(x, *extra)


GAIN_ONE, SHIFT_ONE, DOWN_BIAS, GAIN_TWO, SHIFT_TWO, OUT_BIAS = range(6)


def vector(vec_ref, at):
    return vec_ref[at : at + 1, :]


def first_norm(groups, x_ref, vec_ref, *rest):
    contexts, outs, (h1_ref, n1_ref) = rest[:groups], rest[groups : 2 * groups], rest[2 * groups :]
    h1 = x_ref[...].astype(WIDE) + vector(vec_ref, OUT_BIAS)
    for context, weight in zip(contexts, outs):
        h1 = h1 + dot(context[...], weight[...], NN)
    h1_ref[...] = h1
    hat, _ = stats(h1)
    n1_ref[...] = (hat * vector(vec_ref, GAIN_ONE) + vector(vec_ref, SHIFT_ONE)).astype(LOW)


def call_first_norm(tokens, vec, contexts, packs, block=512):
    count, model = tokens.shape
    groups = len(contexts)
    width = contexts[0].shape[1]
    return pl.pallas_call(
        functools.partial(first_norm, groups),
        grid=(count // block,),
        in_specs=[rows(block, model), whole(vec.shape)]
        + [rows(block, width)] * groups
        + [pl.BlockSpec((width, model), lambda i: (3, 0))] * groups,
        out_specs=[rows(block, model)] * 2,
        out_shape=[jax.ShapeDtypeStruct((count, model), WIDE), jax.ShapeDtypeStruct((count, model), LOW)],
        compiler_params=params(),
        cost_estimate=cost(count),
    )(tokens, vec, *contexts, *packs)


def norm_back(grad, hat, scale, gain):
    d = grad * gain
    first = jnp.mean(d, axis=1, keepdims=True)
    second = jnp.mean(d * hat, axis=1, keepdims=True)
    return scale * (d - first - hat * second)


def column_sum(values):
    return jnp.sum(values, axis=0, keepdims=True)


def back_through(dm, slope, wi_ref, wd_ref, dn1, keep=None):
    chunk = 768
    for c in range(0, wi_ref.shape[0], chunk):
        cols = slice(c, c + chunk)
        dact = dot(dm, wd_ref[cols, :], NT)
        du = (dact * slope[:, cols].astype(WIDE)).astype(LOW)
        if keep is not None:
            keep(cols, du)
        dn1 = dn1 + dot(du, wi_ref[cols, :], NN)
    return dn1


def middle_own(h1_ref, m_ref, cot_ref, vec_ref, slope_ref, wi_ref, wd_ref, act_ref, n1_ref, *outs):
    layer_ref, dm_ref, dn1_ref, sums_ref, down_ref, inner_ref = outs

    @pl.when(pl.program_id(0) == 0)
    def _():
        sums_ref[...] = jnp.zeros_like(sums_ref)
        down_ref[...] = jnp.zeros_like(down_ref)
        inner_ref[...] = jnp.zeros_like(inner_ref)

    hat1, _ = stats(h1_ref[...])
    normed = hat1 * vector(vec_ref, GAIN_ONE) + vector(vec_ref, SHIFT_ONE)
    hat2, scale2 = stats(normed + m_ref[...] + vector(vec_ref, DOWN_BIAS))
    layer_ref[...] = (hat2 * vector(vec_ref, GAIN_TWO) + vector(vec_ref, SHIFT_TWO)).astype(LOW)
    up = cot_ref[...].astype(WIDE)
    sums_ref[0:1, :] += column_sum(up * hat2)
    sums_ref[1:2, :] += column_sum(up)
    dh2 = norm_back(up, hat2, scale2, vector(vec_ref, GAIN_TWO))
    sums_ref[2:3, :] += column_sum(dh2)
    dm = dh2.astype(LOW)
    dm_ref[...] = dm
    down_ref[...] += inner_first(act_ref[...], dm)

    def keep(cols, du):
        inner_ref[:, cols] += inner_first(n1_ref[...], du)
        sums_ref[6:7, cols] += column_sum(du.astype(WIDE))

    dn1_ref[...] = back_through(dm, slope_ref, wi_ref, wd_ref, dh2, keep)


def middle_rest(groups, h1_ref, dn1_ref, dm_ref, vec_ref, old_ref, *rest):
    slopes, wis, wds = rest[:groups], rest[groups : 2 * groups], rest[2 * groups : 3 * groups]
    dh1_ref, da_ref, sums_ref = rest[3 * groups :]

    @pl.when(pl.program_id(0) == 0)
    def _():
        sums_ref[...] = old_ref[...]

    hat1, scale1 = stats(h1_ref[...])
    dm = dm_ref[...]
    dn1 = dn1_ref[...]
    for slope_ref, wi_ref, wd_ref in zip(slopes, wis, wds):
        dn1 = back_through(dm, slope_ref, wi_ref, wd_ref, dn1)
    sums_ref[3:4, :] += column_sum(dn1 * hat1)
    sums_ref[4:5, :] += column_sum(dn1)
    dh1 = norm_back(dn1, hat1, scale1, vector(vec_ref, GAIN_ONE))
    sums_ref[5:6, :] += column_sum(dh1)
    dh1_ref[...] = dh1
    da_ref[...] = dh1.astype(LOW)


def call_middle_own(h1, mixed, cot, vec, slope, wi, wd, act, n1, block=512):
    count, model = h1.shape
    hidden = wi.shape[0]
    once = pl.BlockSpec((hidden, model), lambda i: (0, 0), pipeline_mode=pl.Buffered(1))
    return pl.pallas_call(
        middle_own,
        grid=(count // block,),
        in_specs=[rows(block, model)] * 3 + [whole(vec.shape), rows(block, hidden)] + [once] * 2
        + [rows(block, hidden), rows(block, model)],
        out_specs=[rows(block, model)] * 3 + [whole((8, model)), whole((hidden, model)), whole((model, hidden))],
        out_shape=[
            jax.ShapeDtypeStruct((count, model), LOW),
            jax.ShapeDtypeStruct((count, model), LOW),
            jax.ShapeDtypeStruct((count, model), WIDE),
            jax.ShapeDtypeStruct((8, model), WIDE),
            jax.ShapeDtypeStruct((hidden, model), WIDE),
            jax.ShapeDtypeStruct((model, hidden), WIDE),
        ],
        input_output_aliases={1: 2},
        compiler_params=params(61 * 1024 * 1024),
        cost_estimate=cost(count),
    )(h1, mixed, cot, vec, slope, wi, wd, act, n1)


def call_middle_rest(h1, dn1, dm, vec, sums, slopes, wis, wds, block=512):
    count, model = h1.shape
    groups = len(slopes)
    hidden = wis[0].shape[0]
    once = pl.BlockSpec((hidden, model), lambda i: (0, 0), pipeline_mode=pl.Buffered(1))
    return pl.pallas_call(
        functools.partial(middle_rest, groups),
        grid=(count // block,),
        in_specs=[rows(block, model)] * 3
        + [whole(vec.shape), whole((8, model))]
        + [rows(block, hidden)] * groups
        + [once] * (2 * groups),
        out_specs=[rows(block, model), rows(block, model), whole((8, model))],
        out_shape=[
            jax.ShapeDtypeStruct((count, model), WIDE),
            jax.ShapeDtypeStruct((count, model), LOW),
            jax.ShapeDtypeStruct((8, model), WIDE),
        ],
        input_output_aliases={1: 0},
        compiler_params=params(61 * 1024 * 1024),
        cost_estimate=cost(count),
    )(h1, dn1, dm, vec, sums, *slopes, *wis, *wds)


def inner_first(left, right):
    return lax.dot_general(left, right, (((0,), (0,)), ((), ())), preferred_element_type=WIDE)


def assemble(place_ref, *rest):
    pieces, outs, out_ref = rest[:LANES], rest[LANES:-1], rest[-1]
    part = pieces[0].shape[0]
    core, chip = place_ref[0] % 2, place_ref[0] // 2
    for k, piece in enumerate(pieces):
        half = core if k < 4 else 1 - core
        at = pl.multiple_of((half * 4 + (chip ^ (k % 4))) * part, 8)
        out_ref[pl.ds(at, part), :] = piece[...]
    width = outs[3].shape[0]
    for k in range(4):
        outs[k][...] = out_ref[k * width : (k + 1) * width, :]
    outs[4][...] = out_ref[4 * width : 4 * width + 16, :]


def call_assemble(place, pieces, width):
    part, model = pieces[0].shape
    shapes = [(width, model)] * 4 + [(16, model)]
    return pl.pallas_call(
        assemble,
        grid=(1,),
        in_specs=[pl.BlockSpec(memory_space=pltpu.SMEM)] + [whole((part, model))] * LANES,
        out_specs=[whole(shape) for shape in shapes],
        out_shape=[jax.ShapeDtypeStruct(shape, WIDE) for shape in shapes],
        scratch_shapes=[pltpu.VMEM((part * LANES, model), WIDE)],
        compiler_params=params(),
    )(place, *pieces)


def after(values, *done):
    return lax.optimization_barrier((values, done))[0]


def swap(value, mask, size):
    return lax.ppermute(value, "dp", [(i, i ^ mask) for i in range(size)])


def from_tensor(value, shift, groups):
    return lax.ppermute(value, "tensor", [((i + shift) % groups, i) for i in range(groups)])


class Spread:
    def __init__(self, piece, shift, groups, size):
        self.piece, self.shift, self.groups, self.size = piece, shift, groups, size
        self.got = {}

    def along(self, *done):
        self.got[0] = from_tensor(after(self.piece, *done), self.shift, self.groups)
        return self.got[0]

    def hop(self, m, mask, *done):
        self.got[m ^ mask] = swap(after(self.got[m], *done), mask, self.size)
        return self.got[m ^ mask]

    def slices(self):
        return [self.got[m] for m in range(LANES)]


class Total:
    def __init__(self, value, size):
        self.value, self.size = value, size
        self.me = lax.axis_index("dp")
        self.half = value.shape[0] // 2
        self.part = self.half // 4

    def cut(self, value, at, count):
        return lax.dynamic_slice(value, (at, 0), (count, value.shape[1]))

    def pair(self, *done):
        value = after(self.value, *done)
        core = self.me % 2
        self.kept = self.cut(value, core * self.half, self.half)
        self.come = swap(self.cut(value, (1 - core) * self.half, self.half), 1, self.size)
        return self.come

    def scatter(self, *done):
        half = self.kept + after(self.come, *done)
        spot = (self.me // 2) % 4
        parts = [self.cut(half, (spot ^ m) * self.part, self.part) for m in range(4)]
        self.got = [parts[0]] + [swap(parts[m], 2 * m, self.size) for m in (1, 2, 3)]
        return self.got

    def gather(self, *done):
        a, b, c, d = after(self.got, *done)
        total = (a + b) + (c + d)
        mask = LANES
        while mask < self.size:
            total = total + swap(total, mask, self.size)
            mask *= 2
        self.got = [total] + [swap(total, 2 * m, self.size) for m in (1, 2, 3)]
        self.other = [swap(total, 1, self.size)]
        return self.got + self.other

    def share(self, *done):
        self.got = list(after(self.got, *done))
        self.other += [swap(part, 1, self.size) for part in self.got[1:]]
        return self.other

    def pieces(self):
        return [*self.got, *self.other]


def per_device(
    groups,
    size,
    tokens,
    segments,
    query_weight,
    key_weight,
    value_weight,
    query_bias,
    value_bias,
    output_weight,
    output_bias,
    gain_one,
    shift_one,
    inner_weight,
    inner_bias,
    down_weight,
    down_bias,
    gain_two,
    shift_two,
    cotangent,
):
    count, model = tokens.shape
    width = query_weight.shape[1]
    hidden = inner_weight.shape[1]
    place = (lax.axis_index("dp") % LANES).astype(jnp.int32)
    place_arg = place.reshape(1)
    others = range(1, groups)
    row = lambda v: v.reshape(1, -1)

    qkvo = jnp.concatenate([query_weight.T, key_weight.T, value_weight.T, output_weight], axis=0)
    inner_t = inner_weight.T
    narrow, deep = width // LANES, hidden // LANES

    def bias_rows(values):
        return jnp.pad(row(values), ((0, 7), (0, model - values.shape[0])))

    head_bias = jnp.concatenate([query_bias, jnp.zeros_like(query_bias), value_bias])
    head_piece = jnp.concatenate(
        [
            lax.dynamic_slice(
                qkvo.reshape(4, width, model), (0, place * narrow, 0), (4, narrow, model)
            ).reshape(4 * narrow, model).astype(WIDE),
            bias_rows(head_bias),
        ],
        axis=0,
    )
    deep_piece = jnp.concatenate(
        [
            lax.dynamic_slice(inner_t, (place * deep, 0), (deep, model)).astype(WIDE),
            lax.dynamic_slice(down_weight, (place * deep, 0), (deep, model)).astype(WIDE),
            bias_rows(inner_bias),
        ],
        axis=0,
    )
    vec = jnp.stack([gain_one, shift_one, down_bias, gain_two, shift_two, output_bias, output_bias, output_bias])
    scol = segments.reshape(count, 1)
    srow = segments.reshape(count // SEQ_LEN, 1, SEQ_LEN)

    order = [j for j in others if j % 2] + [j for j in others if j % 2 == 0]
    head_of = [Spread(head_piece, j, groups, size) for j in order]
    deep_of = [Spread(deep_piece, j, groups, size) for j in order]
    saved = {}

    def forward(k, *done):
        if k < 0:
            out = call_attend_forward(
                width, after(tokens, *done), scol, srow, row(head_bias), qkvo, None, None
            )
            saved[0] = (*out, qkvo)
        else:
            slices = after(head_of[k].slices(), *done)
            out = call_attend_forward(width, tokens, scol, srow, None, None, place_arg, slices)
            saved[order[k]] = out
        return out[2]

    a, b, c = head_of
    d, e, f = deep_of
    gate = [a.along()]
    late = c.along(gate)
    gate = [
        a.hop(0, 2, gate), a.hop(0, 4, gate), a.hop(0, 6, gate), b.along(gate), forward(-1, gate, deep_piece)
    ]
    gate = [a.hop(m, 1, gate) for m in (0, 2, 4, 6)] + [late]
    late = d.along(gate)
    gate = [forward(0, gate), b.hop(0, 2, gate), b.hop(0, 4, gate), b.hop(0, 6, gate), b.hop(0, 1, gate)]
    later = e.along(gate)
    gate = [b.hop(m, 1, gate) for m in (2, 4, 6)] + [late]
    gate = [forward(1, gate), c.hop(0, 2, gate), c.hop(0, 4, gate), c.hop(0, 6, gate), c.hop(0, 1, gate), later]
    begun = [d.hop(0, 2, gate), d.hop(0, 4, gate)]
    gate = [c.hop(m, 1, gate) for m in (2, 4, 6)]
    late = [f.along(gate), e.hop(0, 2, gate)]
    gate = [forward(2, gate), begun, d.hop(0, 1, gate)]
    contexts, packs = [saved[j][1] for j in range(groups)], [saved[j][3] for j in range(groups)]
    h1, n1 = call_first_norm(after(tokens, gate), vec, contexts, packs)
    slopes, wis, wds = [], [inner_t], [down_weight]

    def deep_forward(k, mixed, *done):
        slices = after(deep_of[k].slices(), *done)
        slope, mixed, wi, wd = call_feed_forward(hidden, n1, True, (mixed, place_arg, *slices))
        slopes.append(slope)
        wis.append(wi)
        wds.append(wd)
        return slope, mixed

    begun = [d.hop(2, 4, gate), d.hop(2, 1, gate), e.hop(0, 4, gate)]
    gate = [n1, late]
    begun += [f.hop(0, 2, gate), e.hop(0, 1, gate)]
    slope, mixed, act = call_feed_forward(
        hidden, after(n1, gate), False, (row(inner_bias), inner_t, down_weight)
    )
    slopes.append(slope)
    gate = [slope, begun]
    begun = [f.hop(0, 4, gate), e.hop(4, 2, gate), e.hop(2, 1, gate)]
    gate = [d.hop(4, 1, gate), d.hop(6, 1, gate)]
    slope, mixed = deep_forward(0, mixed, gate)
    gate = [slope, begun]
    begun = [f.hop(2, 4, gate), f.hop(0, 1, gate), f.hop(2, 1, gate)]
    gate = [e.hop(4, 1, gate), e.hop(6, 1, gate)]
    slope, mixed = deep_forward(1, mixed, gate)
    gate = [slope, begun]
    gate = [f.hop(4, 1, gate), f.hop(6, 1, gate)]
    slope, mixed = deep_forward(2, mixed, gate)

    layer_out, dm, dn1, sums, *own = call_middle_own(
        h1, mixed, cotangent, vec, slopes[0], wis[0], wds[0], act, n1
    )

    own = after(tuple(own), dm)
    down_grad, inner_grad = lax.psum(own, "dp")
    dh1, da, sums = call_middle_rest(h1, after(dn1, own), dm, vec, sums, slopes[1:], wis[1:], wds[1:])

    def backward(j, *done):
        qkv, context, logs, pack = saved[j]
        return call_attend_backward(j == 0, qkv, context, logs, scol, srow, after(da, *done), pack)

    dqkv0, qkv_sums = backward(0)
    parts = [inner_first(dqkv0, tokens), inner_first(saved[0][1], da), sums, qkv_sums]
    used = sum(part.shape[0] for part in parts)
    parts.append(jnp.zeros((-used % (8 * LANES), model), WIDE))
    heads = Total(jnp.concatenate(parts, axis=0), size)
    gate = [heads.value]
    dqkvs, packs = [dqkv0], [qkvo]
    moved = heads.pair(gate)
    for k, j in enumerate(order):
        (grad,) = backward(j, gate)
        dqkvs.append(grad)
        packs.append(saved[j][3])
        gate = [grad]
        if k == 0:
            gate = [grad, moved]
            moved = heads.scatter(gate)
    gate = [gate, moved]
    moved = heads.gather(gate)
    tokens_grad = call_input_gradient(after(dh1, gate), dqkvs, packs)
    heads.share(tokens_grad)
    query_grad, key_grad, value_grad, output_grad, sums = call_assemble(
        place_arg, heads.pieces(), width
    )
    return (
        layer_out,
        tokens_grad,
        query_grad.T,
        key_grad.T,
        value_grad.T,
        sums[8, :width],
        sums[8, 2 * width : 3 * width],
        output_grad,
        sums[5],
        sums[3],
        sums[4],
        inner_grad,
        sums[6, :hidden],
        down_grad,
        sums[2],
        sums[0],
        sums[1],
    )


def solution(mesh):
    whole_rows, columns, lines, split = P("dp", None), P(None, "tensor"), P("tensor", None), P("tensor")
    in_specs = (
        whole_rows, P("dp"), columns, columns, columns, split, split, lines, P(), P(), P(),
        columns, split, lines, P(), P(), P(), whole_rows,
    )
    out_specs = (
        whole_rows, whole_rows, columns, columns, columns, split, split, lines, P(), P(), P(),
        columns, split, lines, P(), P(), P(),
    )
    body = functools.partial(per_device, mesh.shape["tensor"], mesh.shape["dp"])
    return jax.shard_map(body, mesh=mesh, in_specs=in_specs, out_specs=out_specs, check_vma=False)
```
